32 devices in a mesh: dp: 4 (over y, x), seq: 8 (over z, core).
Axes of the slice: x: 2, y: 2, z: 4, core: 2. Of those that a mesh axis runs over, the one named last changes fastest.
Arguments:
- features: bfloat16 [6144, 1408], P(('dp', 'seq')), parts along dimension 0, may hold values from -6 to 6
- norm_gain: float32 [1408], replicated, may hold values from 0.1 to 1.9
- conv_weight: bfloat16 [5, 1408, 1536], P(None, None, 'seq'), may hold values from -0.0625 to 0.0625
- conv_bias: float32 [1536], replicated, may hold values from -3 to 3
- attn_gain: float32 [1536], replicated, may hold values from 0.1 to 1.9
- query_weight: bfloat16 [1536, 1024], P('seq'), may hold values from -1 to 1
- keyval_weight: bfloat16 [1536, 256], P('seq'), may hold values from -1 to 1
- head_scale: float32 [8], replicated, may hold values from 1 to 4
- output_weight: bfloat16 [1024, 1536], P('seq'), may hold values from -0.1875 to 0.1875
Outputs:
- coarse: bfloat16 [3072, 1536], P(('dp', 'seq')), parts along dimension 0
- attended: bfloat16 [3072, 1536], P(('dp', 'seq')), parts along dimension 0
The draws below stay inside these ranges and needn't reach their ends.
There are 4 independent parts, one for each index of `dp`. The reference program is written for one: setup_inputs(seed, part) draws one part's arguments, and reference() takes and returns one part's arrays. A program takes and returns all parts, laid end to end along the dimension named above; an argument that names none is the same for every part. Nothing has to cross between parts.
All inputs are finite; a program needn't handle non-finite values.
Results may differ from the reference program's by a relative error of at most 0.007.
Values may be sent and summed in bfloat16 or wider, within the bound.
A program may use at most 128 MiB of HBM per device.

```python
import math
import jax
import jax.numpy as jnp
from jax import lax

CH_IN = 1408
CH_OUT = 1536
HEADS = 8
HEAD_DIM = 128
KWIDTH = 5
FINE_LEN = 1536


def shared_weights(key):
    base = jax.random.fold_in(key, 11)
    key_query, key_keyval = jax.random.split(base, 2)
    keyvals = jax.random.normal(key_keyval, (CH_OUT, 2 * HEAD_DIM), jnp.float32) * CH_OUT ** (-0.5)
    noise = jax.random.normal(key_query, (CH_OUT, HEADS, HEAD_DIM), jnp.float32) * CH_OUT ** (-0.5)
    queries = noise
    queries = jnp.clip(queries.reshape(CH_OUT, HEADS * HEAD_DIM), -1.0, 1.0)
    return (queries, jnp.clip(keyvals, -1.0, 1.0))


def draw_query_weight(key, part):
    return shared_weights(key)[0].astype(jnp.bfloat16)


def draw_keyval_weight(key, part):
    return shared_weights(key)[1].astype(jnp.bfloat16)


def shard_levels(rng, extent, cuts, low, top_value):
    factor_of, own = 1.0, jax.random.fold_in(rng, 6)
    for position, shards_of in cuts:
        draws = jnp.exp(jax.random.uniform(jax.random.fold_in(own, position), (shards_of,), jnp.float32, low / len(cuts), top_value / len(cuts)))
        factor_of = factor_of * jnp.repeat(draws, extent[position] // shards_of).reshape([-1 if axis == position else 1 for axis in range(len(extent))])
    return factor_of


def gaussian(key, extent, spread, reach, pieces=(), held_as=jnp.bfloat16):
    result = jax.random.normal(key, extent, jnp.float32) * spread
    if len(pieces) > 0:
        result = shard_levels(key, extent, pieces, -0.22, 0.18) * result
    return jnp.clip(result, min=-reach, max=reach).astype(held_as)


def setup_inputs(seed: int = 0, part: int = 0) -> dict:
    splits = jax.random.split(jax.random.key(seed), 10)
    part_splits = jax.random.split(jax.random.fold_in(splits[9], part), 10)
    return {
        "features": gaussian(part_splits[0], (FINE_LEN, CH_IN), 1.0, 6.0, ((0, 8),)),
        "norm_gain": jnp.clip(1.0 + 0.18 * jax.random.normal(splits[1], (CH_IN,), jnp.float32), 0.1, 1.9),
        "conv_weight": gaussian(splits[2], (KWIDTH, CH_IN, CH_OUT), (KWIDTH * CH_IN) ** -0.5, 0.0625, ((2, 8),)),
        "conv_bias": gaussian(splits[3], (CH_OUT,), 0.5, 3.0, (), jnp.float32),
        "attn_gain": jnp.clip(1.0 + 0.18 * jax.random.normal(splits[4], (CH_OUT,), jnp.float32), 0.1, 1.9),
        "query_weight": draw_query_weight(jax.random.fold_in(splits[9], 71), part),
        "keyval_weight": draw_keyval_weight(jax.random.fold_in(splits[9], 71), part),
        "head_scale": jnp.clip(jnp.exp(jax.random.uniform(splits[7], (HEADS,), jnp.float32, math.log(1.0), math.log(4.0))), 1.0, 4.0),
        "output_weight": gaussian(splits[8], (HEADS * HEAD_DIM, CH_OUT), (HEADS * HEAD_DIM) ** -0.5, 0.1875, ((0, 8),)),
    }


def normalize(values_in, channel_gain):
    meansq = lax.optimization_barrier(jnp.mean(values_in * values_in, axis=-1, keepdims=True))
    return values_in * lax.rsqrt(meansq + 1e-06) * channel_gain

def reference(features, norm_gain, conv_weight, conv_bias, attn_gain, query_weight, keyval_weight, head_scale, output_weight):
    normed = jax.nn.gelu(normalize(features.astype(jnp.float32), norm_gain)).astype(jnp.bfloat16)
    row_count = normed.shape[0]
    padded = jnp.pad(normed, ((2, 2), (0, 0)))
    summed = jnp.zeros((row_count, conv_weight.shape[2]), jnp.float32)
    for kernel_tap in range(KWIDTH):
        summed = summed + jnp.dot(padded[kernel_tap:kernel_tap + row_count], conv_weight[kernel_tap], preferred_element_type=jnp.float32)
    levels = summed + conv_bias[None, :]
    coarse = lax.optimization_barrier(jnp.max(levels.reshape(-1, 2, levels.shape[1]), axis=1)).astype(jnp.bfloat16)
    attn_in = normalize(coarse.astype(jnp.float32), attn_gain).astype(jnp.bfloat16)
    queries = jnp.dot(attn_in, query_weight, preferred_element_type=jnp.float32).astype(jnp.bfloat16)
    keyvals = jnp.dot(attn_in, keyval_weight, preferred_element_type=jnp.float32).astype(jnp.bfloat16)
    keys_all = keyvals[:, :HEAD_DIM]
    values_all = keyvals[:, HEAD_DIM:]
    positions = queries.shape[0]
    head_queries = queries.reshape(positions, HEADS, HEAD_DIM).transpose(1, 0, 2)

    def one_head(operands):
        head_query, scale_one = operands
        scores = jnp.dot(head_query, keys_all.T, preferred_element_type=jnp.float32) * scale_one * HEAD_DIM ** (-0.5)
        biggest = lax.optimization_barrier(jnp.max(scores, axis=1, keepdims=True))
        expon = jnp.exp(scores - biggest)
        denom = lax.optimization_barrier(jnp.sum(expon, axis=1, keepdims=True))
        return jnp.dot(expon.astype(jnp.bfloat16), values_all, preferred_element_type=jnp.float32) / denom
    contexts = lax.map(one_head, (head_queries, head_scale))
    context = contexts.transpose(1, 0, 2).reshape(positions, HEADS * HEAD_DIM).astype(jnp.bfloat16)
    attended = jnp.dot(context, output_weight, preferred_element_type=jnp.float32).astype(jnp.bfloat16)
    return (coarse, attended)
```

```python
import jax
import jax.numpy as jnp
from jax import lax
from jax.sharding import PartitionSpec as P

HEAD_DIM = 128


def with_halo(block, sides, width):
    for axis, dim in sides:
        count = lax.axis_size(axis)
        forward = [(i, i + 1) for i in range(count - 1)]
        backward = [(target, source) for source, target in forward]
        low = lax.ppermute(
            lax.slice_in_dim(block, block.shape[dim] - width, None, axis=dim), axis, forward
        )
        high = lax.ppermute(lax.slice_in_dim(block, 0, width, axis=dim), axis, backward)
        block = jnp.concatenate([low, block, high], axis=dim)
    return block


def normalize(values_in, channel_gain):
    meansq = jnp.mean(values_in * values_in, axis=-1, keepdims=True)
    return values_in * lax.rsqrt(meansq + 1e-06) * channel_gain


def convolve(padded, kernel, row_count):
    summed = jnp.zeros((row_count, kernel.shape[2]), jnp.float32)
    for kernel_tap in range(kernel.shape[0]):
        summed = summed + jnp.dot(
            padded[kernel_tap : kernel_tap + row_count],
            kernel[kernel_tap],
            preferred_element_type=jnp.float32,
        )
    return summed


def pool_pairs(levels):
    return jnp.max(levels.reshape(-1, 2, levels.shape[1]), axis=1)


def attend(queries, keyvals, scales):
    row_count = queries.shape[0]
    head_count = scales.shape[0]
    shaped = queries.reshape(row_count, head_count, HEAD_DIM)
    key_block = lax.all_gather(keyvals, "seq", axis=0, tiled=True)
    running_max = jnp.full((head_count, row_count), -1e30, jnp.float32)
    key_part = key_block[:, :HEAD_DIM]
    value_part = key_block[:, HEAD_DIM:]
    scores = (
        jnp.einsum("qhd,kd->hqk", shaped, key_part, preferred_element_type=jnp.float32)
        * scales[:, None, None]
        * HEAD_DIM ** (-0.5)
    )
    newest = jnp.maximum(running_max, jnp.max(scores, axis=2))
    expon = jnp.exp(scores - newest[:, :, None])
    running_sum = jnp.sum(expon, axis=2)
    running_ctx = jnp.einsum(
        "hqk,kd->hqd", expon.astype(jnp.bfloat16), value_part, preferred_element_type=jnp.float32
    )
    context = running_ctx / running_sum[:, :, None]
    return context.transpose(1, 0, 2).reshape(row_count, head_count * HEAD_DIM).astype(jnp.bfloat16)


def shards(
    features,
    norm_gain,
    conv_weight,
    conv_bias,
    attn_gain,
    query_weight,
    keyval_weight,
    head_scale,
    output_weight,
):
    normed = jax.nn.gelu(normalize(features.astype(jnp.float32), norm_gain)).astype(jnp.bfloat16)
    window = lax.all_gather(normed, "seq", axis=0, tiled=True)
    fine_rows = window.shape[0]
    width = conv_weight.shape[0] // 2
    padded = jnp.pad(window, ((width, width), (0, 0)))
    channels = conv_weight.shape[2]
    own_bias = lax.dynamic_slice_in_dim(conv_bias, lax.axis_index("seq") * channels, channels)
    levels = convolve(padded, conv_weight, fine_rows) + own_bias[None, :]
    pooled = pool_pairs(levels).astype(jnp.bfloat16)
    coarse = lax.all_to_all(pooled, "seq", split_axis=0, concat_axis=1, tiled=True)
    attn_in = normalize(coarse.astype(jnp.float32), attn_gain).astype(jnp.bfloat16)
    columns = attn_in
    query_sum = jnp.dot(
        columns,
        lax.all_gather(query_weight, "seq", axis=0, tiled=True),
        preferred_element_type=jnp.float32,
    )
    keyval_sum = jnp.dot(
        columns,
        lax.all_gather(keyval_weight, "seq", axis=0, tiled=True),
        preferred_element_type=jnp.float32,
    )
    queries = query_sum.astype(jnp.bfloat16)
    keyvals = keyval_sum.astype(jnp.bfloat16)
    context = attend(queries, keyvals, head_scale)
    columns = context
    projected = jnp.dot(
        columns,
        lax.all_gather(output_weight, "seq", axis=0, tiled=True),
        preferred_element_type=jnp.float32,
    )
    return (coarse, projected.astype(jnp.bfloat16))


def solution(mesh):
    return jax.shard_map(
        shards,
        mesh=mesh,
        in_specs=(
            P(("dp", "seq"), None),
            P(),
            P(None, None, "seq"),
            P(),
            P(),
            P("seq", None),
            P("seq", None),
            P(),
            P("seq", None),
        ),
        out_specs=(P(("dp", "seq"), None), P(("dp", "seq"), None)),
        check_vma=False,
    )
```

```python
import jax
import jax.numpy as jnp
from jax import lax
from jax.experimental import pallas as pl
from jax.experimental.pallas import tpu as pltpu
from jax.sharding import PartitionSpec as P

HEAD_DIM = 128
MESH = pl.DeviceIdType.MESH
MARGIN = 16
EDGE = 8


def flip(a, b):
    low = lax.rem(lax.rem(a, 2) + lax.rem(b, 2), 2)
    high = lax.rem(lax.div(a, 2) + lax.div(b, 2), 2)
    return low + 2 * high


def fused_kernel(
    feat_ref, ngain_ref, cw_ref, bias_ref, again_ref, wq_ref, wkv_ref, scale_ref, wo_ref,
    coarse_ref, attended_ref,
    win, tmp0, tmp1, acc0, acc1, csend, cbuf, wqkv, wout, kvbuf,
    act_send, act_recv, wa_send, wa_recv, wb_send, wb_recv, wc_send, wc_recv,
    co_send, co_recv, kv_send, kv_recv,
):
    p = lax.axis_index("dp")
    s = lax.axis_index("seq")
    z, c = lax.div(s, 2), lax.rem(s, 2)
    other = 1 - c
    sibling = (p, 2 * z + other)
    block = feat_ref.shape[0]
    half = block // 2
    heads = scale_ref.shape[0]
    qcols = wq_ref.shape[1]
    taps = cw_ref.shape[0]
    width = cw_ref.shape[2]
    depth = wq_ref.shape[0] // 4
    odepth = wo_ref.shape[0] // 4

    def remote(src, dst, send, recv, device):
        return pltpu.make_async_remote_copy(
            src_ref=src, dst_ref=dst, send_sem=send, recv_sem=recv,
            device_id=device, device_id_type=MESH,
        )

    barrier = pltpu.get_barrier_semaphore()
    for k in range(1, 8):
        pl.semaphore_signal(
            barrier, inc=1, device_id=(p, lax.rem(s + k, 8)), device_id_type=MESH
        )
    for k in range(1, 4):
        pl.semaphore_signal(
            barrier, inc=1, device_id=(lax.rem(p + k, 4), s), device_id_type=MESH
        )
    wqkv[c, z, :, :qcols] = wq_ref[...]
    wqkv[c, z, :, qcols:] = wkv_ref[...]
    wout[c, z] = wo_ref[...]
    pl.semaphore_wait(barrier, 10)

    started = []

    def qkv_part(cc, zz, pp):
        return wqkv.at[cc, zz, pl.ds(pl.multiple_of(pp * depth, 16), depth), :]

    def out_part(cc, zz, pp):
        return wout.at[cc, zz, pl.ds(pl.multiple_of(pp * odepth, 16), odepth), :]

    for k in range(1, 4):
        peer = (p, 2 * flip(z, k) + c)
        for n, part in enumerate((qkv_part, out_part)):
            copy = remote(
                part(c, z, p), part(c, z, p), wa_send.at[n, k], wa_recv.at[n, z], peer
            )
            copy.start()
            started.append(copy)

    x = feat_ref[...].astype(jnp.float32)
    meansq = jnp.mean(x * x, axis=-1, keepdims=True)
    normed = x * lax.rsqrt(meansq + 1e-06) * ngain_ref[...]
    win[s] = jax.nn.gelu(normed).astype(jnp.bfloat16)
    for k in range(1, 4):
        copy = remote(
            win.at[s], win.at[s], act_send.at[k], act_recv.at[s], (p, 2 * flip(z, k) + c)
        )
        copy.start()
        started.append(copy)
    copy = remote(win.at[s], win.at[s], act_send.at[0], act_recv.at[s], sibling)
    copy.start()
    started.append(copy)

    acc0[...] = jnp.zeros_like(acc0)
    acc1[...] = jnp.zeros_like(acc1)
    tmp0[...] = jnp.zeros_like(tmp0)
    tmp1[...] = jnp.zeros_like(tmp1)

    def convolve_block(b):
        rows = win[b]
        for t in range(taps):
            y = jnp.dot(rows, cw_ref[t], preferred_element_type=jnp.float32)
            tmp0[t, MARGIN : MARGIN + block, :] = y[:, :128]
            tmp1[t, MARGIN : MARGIN + block, : width - 128] = y[:, 128:]
        span = block + 2 * EDGE
        first = MARGIN - EDGE - taps // 2
        at = pl.ds(pl.multiple_of(b * block, 8), span)
        for tmp, acc in ((tmp0, acc0), (tmp1, acc1)):
            total = tmp[0, first : first + span, :]
            for t in range(1, taps):
                total = total + tmp[t, first + t : first + t + span, :]
            acc[at, :] += total

    def wait_block(b):
        remote(win.at[b], win.at[b], act_send.at[0], act_recv.at[b], sibling).wait_recv()

    convolve_block(s)
    for k in range(1, 4):
        zz = flip(z, k)
        for n, part in enumerate((qkv_part, out_part)):
            here = part(c, zz, p)
            remote(here, here, wa_send.at[n, 0], wa_recv.at[n, zz], sibling).wait_recv()
            for m in range(1, 4):
                copy = remote(
                    here, here, wb_send.at[n, k, m], wb_recv.at[n, zz, p],
                    (lax.rem(p + m, 4), s),
                )
                copy.start()
                started.append(copy)

    def step(k, carry):
        zz = flip(z, k)

        @pl.when(k > 0)
        def _():
            b = 2 * zz + c
            wait_block(b)
            remote(
                win.at[b], win.at[b], act_send.at[3 + k], act_recv.at[b], sibling
            ).start()
            convolve_block(b)

        b = 2 * zz + other
        wait_block(b)
        convolve_block(b)
        return carry

    lax.fori_loop(0, 4, step, 0)

    bias = bias_ref[s]

    def pooled(r, out):
        start = pl.multiple_of(r * block, 8) + EDGE
        c0 = jnp.maximum(
            acc0[pl.ds(start, half, stride=2), :], acc0[pl.ds(start + 1, half, stride=2), :]
        )
        c1 = jnp.maximum(
            acc1[pl.ds(start, half, stride=2), :], acc1[pl.ds(start + 1, half, stride=2), :]
        )
        out[:, :128] = (c0 + bias[:, :128]).astype(jnp.bfloat16)
        out[:, 128:] = (c1[:, : width - 128] + bias[:, 128:]).astype(jnp.bfloat16)

    for k in range(1, 8):
        r = lax.rem(s + k, 8)
        pooled(r, csend.at[r])
        copy = remote(csend.at[r], cbuf.at[s], co_send.at[k], co_recv.at[s], (p, r))
        copy.start()
        started.append(copy)
    pooled(s, cbuf.at[s])

    for k in range(1, 4):
        zz = flip(z, k)
        for n, part in enumerate((qkv_part, out_part)):
            for m in range(1, 4):
                pp = lax.rem(p + m, 4)
                there = part(c, zz, pp)
                remote(
                    there, there, wa_send.at[n, 0], wb_recv.at[n, zz, pp], sibling
                ).wait_recv()
    for n, full in enumerate((wqkv, wout)):
        copy = remote(full.at[c], full.at[c], wc_send.at[n], wc_recv.at[n], sibling)
        copy.start()
        started.append(copy)

    for k in range(1, 8):
        r = lax.rem(s + k, 8)
        remote(csend.at[r], cbuf.at[r], co_send.at[0], co_recv.at[r], sibling).wait_recv()

    squares = jnp.zeros((half, 1), jnp.float32)
    for j in range(8):
        piece = cbuf[j].astype(jnp.float32)
        squares = squares + jnp.sum(piece * piece, axis=-1, keepdims=True)
        coarse_ref[j] = cbuf[j]
    inverse = lax.rsqrt(squares / (8 * width) + 1e-06)

    remote(
        wqkv.at[other], wqkv.at[other], wc_send.at[0], wc_recv.at[0], sibling
    ).wait_recv()
    attn = []
    kv = jnp.zeros((half, wkv_ref.shape[1]), jnp.float32)
    for j in range(8):
        piece = (cbuf[j].astype(jnp.float32) * inverse * again_ref[j]).astype(jnp.bfloat16)
        attn.append(piece)
        kv = kv + jnp.dot(
            piece, wqkv[j % 2, j // 2, :, qcols:], preferred_element_type=jnp.float32
        )
    kvbuf[s] = kv.astype(jnp.bfloat16)
    for k in range(1, 8):
        copy = remote(
            kvbuf.at[s], kvbuf.at[s], kv_send.at[k], kv_recv.at[s], (p, lax.rem(s + k, 8))
        )
        copy.start()
        started.append(copy)
    query = jnp.zeros((half, qcols), jnp.float32)
    for j in range(8):
        query = query + jnp.dot(
            attn[j], wqkv[j % 2, j // 2, :, :qcols], preferred_element_type=jnp.float32
        )
    query = query.astype(jnp.bfloat16)
    remote(
        wout.at[other], wout.at[other], wc_send.at[1], wc_recv.at[1], sibling
    ).wait_recv()
    for k in range(1, 8):
        r = lax.rem(s + k, 8)
        remote(kvbuf.at[r], kvbuf.at[r], kv_send.at[0], kv_recv.at[r], sibling).wait_recv()

    keyvals = kvbuf[...].reshape(8 * half, kvbuf.shape[2])
    keys, values = keyvals[:, :HEAD_DIM], keyvals[:, HEAD_DIM:]
    result = jnp.zeros(attended_ref.shape, jnp.float32)
    for h in range(heads):
        scores = lax.dot_general(
            query[:, h * HEAD_DIM : (h + 1) * HEAD_DIM], keys, (((1,), (1,)), ((), ())),
            preferred_element_type=jnp.float32,
        ) * (scale_ref[h] * HEAD_DIM ** (-0.5))
        expon = jnp.exp(scores - jnp.max(scores, axis=1, keepdims=True))
        denom = jnp.sum(expon, axis=1, keepdims=True)
        context = jnp.dot(
            expon.astype(jnp.bfloat16), values, preferred_element_type=jnp.float32
        )
        context = (context / denom).astype(jnp.bfloat16)
        result = result + jnp.dot(
            context, wout[h % 2, h // 2], preferred_element_type=jnp.float32
        )
    attended_ref[...] = result.astype(jnp.bfloat16)

    for copy in started:
        copy.wait_send()
    for k in range(1, 4):
        b = 2 * flip(z, k) + c
        remote(
            win.at[b], win.at[b], act_send.at[3 + k], act_recv.at[b], sibling
        ).wait_send()


def fused(
    features, norm_gain, conv_weight, conv_bias, attn_gain,
    query_weight, keyval_weight, head_scale, output_weight,
):
    block, channels = features.shape
    half = block // 2
    taps, _, width = conv_weight.shape
    total = 8 * width
    rows = 8 * block + 2 * EDGE
    qkv_cols = query_weight.shape[1] + keyval_weight.shape[1]
    f32, bf16 = jnp.float32, jnp.bfloat16
    dma = pltpu.SemaphoreType.DMA
    vmem = pl.BlockSpec(memory_space=pltpu.VMEM)
    smem = pl.BlockSpec(memory_space=pltpu.SMEM)
    coarse, attended = pl.pallas_call(
        fused_kernel,
        out_shape=(
            jax.ShapeDtypeStruct((8, half, width), bf16),
            jax.ShapeDtypeStruct((half, total), bf16),
        ),
        in_specs=[vmem] * 7 + [smem, vmem],
        out_specs=(vmem, vmem),
        scratch_shapes=[
            pltpu.VMEM((8, block, channels), bf16),
            pltpu.VMEM((taps, block + 2 * MARGIN, 128), f32),
            pltpu.VMEM((taps, block + 2 * MARGIN, 128), f32),
            pltpu.VMEM((rows, 128), f32),
            pltpu.VMEM((rows, 128), f32),
            pltpu.VMEM((8, half, width), bf16),
            pltpu.VMEM((8, half, width), bf16),
            pltpu.VMEM((2, 4, query_weight.shape[0], qkv_cols), bf16),
            pltpu.VMEM((2, 4) + output_weight.shape, bf16),
            pltpu.VMEM((8, half, keyval_weight.shape[1]), bf16),
            dma((7,)), dma((8,)),
            dma((2, 4)), dma((2, 4)),
            dma((2, 4, 4)), dma((2, 4, 4)),
            dma((2,)), dma((2,)),
            dma((8,)), dma((8,)),
            dma((8,)), dma((8,)),
        ],
        compiler_params=pltpu.CompilerParams(
            collective_id=0, has_side_effects=True, vmem_limit_bytes=48 * 1024 * 1024
        ),
    )(
        features,
        norm_gain.reshape(1, channels),
        conv_weight,
        conv_bias.reshape(8, 1, width),
        attn_gain.reshape(8, 1, width),
        query_weight,
        keyval_weight,
        head_scale,
        output_weight,
    )
    return coarse.transpose(1, 0, 2).reshape(half, total), attended


def normalize(values_in, channel_gain):
    meansq = jnp.mean(values_in * values_in, axis=-1, keepdims=True)
    return values_in * lax.rsqrt(meansq + 1e-06) * channel_gain


def convolve(padded, kernel, row_count):
    summed = jnp.zeros((row_count, kernel.shape[2]), jnp.float32)
    for kernel_tap in range(kernel.shape[0]):
        summed = summed + jnp.dot(
            padded[kernel_tap : kernel_tap + row_count],
            kernel[kernel_tap],
            preferred_element_type=jnp.float32,
        )
    return summed


def pool_pairs(levels):
    return jnp.max(levels.reshape(-1, 2, levels.shape[1]), axis=1)


def attend(queries, keyvals, scales):
    row_count = queries.shape[0]
    head_count = scales.shape[0]
    shaped = queries.reshape(row_count, head_count, HEAD_DIM)
    key_block = lax.all_gather(keyvals, "seq", axis=0, tiled=True)
    running_max = jnp.full((head_count, row_count), -1e30, jnp.float32)
    key_part = key_block[:, :HEAD_DIM]
    value_part = key_block[:, HEAD_DIM:]
    scores = (
        jnp.einsum("qhd,kd->hqk", shaped, key_part, preferred_element_type=jnp.float32)
        * scales[:, None, None]
        * HEAD_DIM ** (-0.5)
    )
    newest = jnp.maximum(running_max, jnp.max(scores, axis=2))
    expon = jnp.exp(scores - newest[:, :, None])
    running_sum = jnp.sum(expon, axis=2)
    running_ctx = jnp.einsum(
        "hqk,kd->hqd", expon.astype(jnp.bfloat16), value_part, preferred_element_type=jnp.float32
    )
    context = running_ctx / running_sum[:, :, None]
    return context.transpose(1, 0, 2).reshape(row_count, head_count * HEAD_DIM).astype(jnp.bfloat16)


def shards(
    features,
    norm_gain,
    conv_weight,
    conv_bias,
    attn_gain,
    query_weight,
    keyval_weight,
    head_scale,
    output_weight,
):
    normed = jax.nn.gelu(normalize(features.astype(jnp.float32), norm_gain)).astype(jnp.bfloat16)
    window = lax.all_gather(normed, "seq", axis=0, tiled=True)
    fine_rows = window.shape[0]
    width = conv_weight.shape[0] // 2
    padded = jnp.pad(window, ((width, width), (0, 0)))
    channels = conv_weight.shape[2]
    own_bias = lax.dynamic_slice_in_dim(conv_bias, lax.axis_index("seq") * channels, channels)
    levels = convolve(padded, conv_weight, fine_rows) + own_bias[None, :]
    pooled = pool_pairs(levels).astype(jnp.bfloat16)
    coarse = lax.all_to_all(pooled, "seq", split_axis=0, concat_axis=1, tiled=True)
    attn_in = normalize(coarse.astype(jnp.float32), attn_gain).astype(jnp.bfloat16)
    columns = attn_in
    query_sum = jnp.dot(
        columns,
        lax.all_gather(query_weight, "seq", axis=0, tiled=True),
        preferred_element_type=jnp.float32,
    )
    keyval_sum = jnp.dot(
        columns,
        lax.all_gather(keyval_weight, "seq", axis=0, tiled=True),
        preferred_element_type=jnp.float32,
    )
    queries = query_sum.astype(jnp.bfloat16)
    keyvals = keyval_sum.astype(jnp.bfloat16)
    context = attend(queries, keyvals, head_scale)
    columns = context
    projected = jnp.dot(
        columns,
        lax.all_gather(output_weight, "seq", axis=0, tiled=True),
        preferred_element_type=jnp.float32,
    )
    return (coarse, projected.astype(jnp.bfloat16))


def solution(mesh):
    fits = mesh.shape["dp"] == 4 and mesh.shape["seq"] == 8
    return jax.shard_map(
        fused if fits else shards,
        mesh=mesh,
        in_specs=(
            P(("dp", "seq"), None),
            P(),
            P(None, None, "seq"),
            P(),
            P(),
            P("seq", None),
            P("seq", None),
            P(),
            P("seq", None),
        ),
        out_specs=(P(("dp", "seq"), None), P(("dp", "seq"), None)),
        check_vma=False,
    )
```

```python
import jax
import jax.numpy as jnp
from jax import lax
from jax.experimental import pallas as pl
from jax.experimental.pallas import tpu as pltpu
from jax.sharding import PartitionSpec as P

HEAD_DIM = 128
MESH = pl.DeviceIdType.MESH
MARGIN = 16
EDGE = 8


def flip(a, b):
    low = lax.rem(lax.rem(a, 2) + lax.rem(b, 2), 2)
    high = lax.rem(lax.div(a, 2) + lax.div(b, 2), 2)
    return low + 2 * high


def fused_kernel(
    feat_ref, ngain_ref, cw_ref, bias_ref, again_ref, wq_ref, wkv_ref, scale_ref, wo_ref,
    coarse_ref, attended_ref,
    win, tmp0, tmp1, acc0, acc1, csend, cbuf, wqkv, wout, kvbuf,
    bias8, again8, cw, scores_ref, prob_ref, cw_sem, act_send, act_recv, wa_send, wa_recv, wb_send, wb_recv, wc_send, wc_recv,
    co_send, co_recv, kv_send, kv_recv,
):
    p = lax.axis_index("dp")
    s = lax.axis_index("seq")
    z, c = lax.div(s, 2), lax.rem(s, 2)
    other = 1 - c
    sibling = (p, 2 * z + other)
    block = feat_ref.shape[0]
    half = block // 2
    heads = scale_ref.shape[0]
    qcols = wq_ref.shape[1]
    taps = cw_ref.shape[0]
    width = cw_ref.shape[1]
    depth = wq_ref.shape[0] // 4
    odepth = wo_ref.shape[0] // 4

    def remote(src, dst, send, recv, device):
        return pltpu.make_async_remote_copy(
            src_ref=src, dst_ref=dst, send_sem=send, recv_sem=recv,
            device_id=device, device_id_type=MESH,
        )

    load = pltpu.make_async_copy(cw_ref, cw, cw_sem)
    load.start()
    barrier = pltpu.get_barrier_semaphore()
    for k in range(1, 8):
        pl.semaphore_signal(
            barrier, inc=1, device_id=(p, lax.rem(s + k, 8)), device_id_type=MESH
        )
    for k in range(1, 4):
        pl.semaphore_signal(
            barrier, inc=1, device_id=(lax.rem(p + k, 4), s), device_id_type=MESH
        )
    wqkv[c, z, :, :qcols] = wq_ref[...]
    wqkv[c, z, :, qcols:] = wkv_ref[...]
    wout[c, z] = wo_ref[...]
    pl.semaphore_wait(barrier, 10)

    started = []

    def qkv_part(cc, zz, pp):
        return wqkv.at[cc, zz, pl.ds(pl.multiple_of(pp * depth, 16), depth), :]

    def out_part(cc, zz, pp):
        return wout.at[cc, zz, pl.ds(pl.multiple_of(pp * odepth, 16), odepth), :]

    parts = (qkv_part, out_part)

    def along_z(n):
        here = parts[n](c, z, p)
        for k in range(1, 4):
            copy = remote(
                here, here, wa_send.at[n, k], wa_recv.at[n, z], (p, 2 * flip(z, k) + c)
            )
            copy.start()
            started.append(copy)

    def along_dp(n):
        for k in range(1, 4):
            zz = flip(z, k)
            here = parts[n](c, zz, p)
            remote(here, here, wa_send.at[n, 0], wa_recv.at[n, zz], sibling).wait_recv()
            for m in range(1, 4):
                copy = remote(
                    here, here, wb_send.at[n, k, m], wb_recv.at[n, zz, p],
                    (lax.rem(p + m, 4), s),
                )
                copy.start()
                started.append(copy)

    def along_core(n):
        for k in range(1, 4):
            zz = flip(z, k)
            for m in range(1, 4):
                pp = lax.rem(p + m, 4)
                there = parts[n](c, zz, pp)
                remote(
                    there, there, wa_send.at[n, 0], wb_recv.at[n, zz, pp], sibling
                ).wait_recv()
        half_of = (wqkv, wout)[n].at[c]
        copy = remote(half_of, half_of, wc_send.at[n], wc_recv.at[n], sibling)
        copy.start()
        started.append(copy)

    along_z(0)

    x = feat_ref[...].astype(jnp.float32)
    meansq = jnp.mean(x * x, axis=-1, keepdims=True)
    normed = x * lax.rsqrt(meansq + 1e-06) * ngain_ref[...][None, :]
    win[s] = jax.nn.gelu(normed).astype(jnp.bfloat16)
    for k in range(1, 4):
        copy = remote(
            win.at[s], win.at[s], act_send.at[k], act_recv.at[s], (p, 2 * flip(z, k) + c)
        )
        copy.start()
        started.append(copy)
    copy = remote(win.at[s], win.at[s], act_send.at[0], act_recv.at[s], sibling)
    copy.start()
    started.append(copy)

    acc0[...] = jnp.zeros_like(acc0)
    acc1[...] = jnp.zeros_like(acc1)
    tmp0[...] = jnp.zeros_like(tmp0)
    tmp1[...] = jnp.zeros_like(tmp1)

    def convolve_pair(zz):
        rows = win[pl.ds(2 * zz, 2)].reshape(2 * block, win.shape[2])
        for t in range(taps):
            y = lax.dot_general(
                rows, cw[t], (((1,), (1,)), ((), ())), preferred_element_type=jnp.float32
            )
            tmp0[t, MARGIN : MARGIN + 2 * block, :] = y[:, :128]
            tmp1[t, MARGIN : MARGIN + 2 * block, : width - 128] = y[:, 128:]
        span = 2 * block + 2 * EDGE
        first = MARGIN - EDGE - taps // 2
        at = pl.ds(pl.multiple_of(zz * 2 * block, 8), span)
        for tmp, acc in ((tmp0, acc0), (tmp1, acc1)):
            total = tmp[0, first : first + span, :]
            for t in range(1, taps):
                total = total + tmp[t, first + t : first + t + span, :]
            acc[at, :] += total

    def wait_block(b):
        remote(win.at[b], win.at[b], act_send.at[0], act_recv.at[b], sibling).wait_recv()

    load.wait()
    bias_row, again_row = bias_ref[...][None, :], again_ref[...][None, :]
    for j in range(8):
        bias8[j] = bias_row[:, j * width : (j + 1) * width]
        again8[j] = again_row[:, j * width : (j + 1) * width]

    def step(k, carry):
        zz = flip(z, k)

        @pl.when(k > 0)
        def _():
            b = 2 * zz + c
            wait_block(b)
            remote(
                win.at[b], win.at[b], act_send.at[3 + k], act_recv.at[b], sibling
            ).start()

        wait_block(2 * zz + other)
        convolve_pair(zz)
        return carry

    lax.fori_loop(0, 1, step, 0)
    along_dp(0)
    lax.fori_loop(1, 3, step, 0)
    along_z(1)
    along_core(0)
    lax.fori_loop(3, 4, step, 0)

    bias = bias8[s]

    def pooled(r, out):
        start = pl.multiple_of(r * block, 8) + EDGE
        c0 = jnp.maximum(
            acc0[pl.ds(start, half, stride=2), :], acc0[pl.ds(start + 1, half, stride=2), :]
        )
        c1 = jnp.maximum(
            acc1[pl.ds(start, half, stride=2), :], acc1[pl.ds(start + 1, half, stride=2), :]
        )
        out[:, :128] = (c0 + bias[:, :128]).astype(jnp.bfloat16)
        out[:, 128:] = (c1[:, : width - 128] + bias[:, 128:]).astype(jnp.bfloat16)

    for k in range(1, 8):
        r = lax.rem(s + k, 8)
        pooled(r, csend.at[r])
        copy = remote(csend.at[r], cbuf.at[s], co_send.at[k], co_recv.at[s], (p, r))
        copy.start()
        started.append(copy)
    pooled(s, cbuf.at[s])

    along_dp(1)
    for k in range(1, 8):
        r = lax.rem(s + k, 8)
        remote(csend.at[r], cbuf.at[r], co_send.at[0], co_recv.at[r], sibling).wait_recv()

    squares = jnp.zeros((half, 1), jnp.float32)
    for j in range(8):
        piece = cbuf[j].astype(jnp.float32)
        squares = squares + jnp.sum(piece * piece, axis=-1, keepdims=True)
        coarse_ref[j] = cbuf[j]
    inverse = lax.rsqrt(squares / (8 * width) + 1e-06)

    remote(
        wqkv.at[other], wqkv.at[other], wc_send.at[0], wc_recv.at[0], sibling
    ).wait_recv()
    attn = []
    kv = jnp.zeros((half, wkv_ref.shape[1]), jnp.float32)
    for j in range(8):
        piece = (cbuf[j].astype(jnp.float32) * inverse * again8[j]).astype(jnp.bfloat16)
        attn.append(piece)
        kv = kv + jnp.dot(
            piece, wqkv[j % 2, j // 2, :, qcols:], preferred_element_type=jnp.float32
        )
    kvbuf[s] = kv.astype(jnp.bfloat16)
    for k in range(1, 4):
        copy = remote(
            kvbuf.at[s], kvbuf.at[s], kv_send.at[k], kv_recv.at[s], (p, 2 * flip(z, k) + c)
        )
        copy.start()
        started.append(copy)
    copy = remote(kvbuf.at[s], kvbuf.at[s], kv_send.at[0], kv_recv.at[s], sibling)
    copy.start()
    started.append(copy)
    query = jnp.zeros((half, qcols), jnp.float32)
    for j in range(8):
        query = query + jnp.dot(
            attn[j], wqkv[j % 2, j // 2, :, :qcols], preferred_element_type=jnp.float32
        )
    query = query.astype(jnp.bfloat16)
    stacked = jnp.concatenate(
        [query[:, h * HEAD_DIM : (h + 1) * HEAD_DIM] for h in range(heads)], axis=0
    )
    for k in range(1, 4):
        b = 2 * flip(z, k) + c
        remote(kvbuf.at[b], kvbuf.at[b], kv_send.at[0], kv_recv.at[b], sibling).wait_recv()
        copy = remote(kvbuf.at[b], kvbuf.at[b], kv_send.at[3 + k], kv_recv.at[b], sibling)
        copy.start()
        started.append(copy)
    along_core(1)
    for k in range(4):
        b = 2 * flip(z, k) + other
        remote(kvbuf.at[b], kvbuf.at[b], kv_send.at[0], kv_recv.at[b], sibling).wait_recv()

    keyvals = kvbuf[...].reshape(8 * half, kvbuf.shape[2])
    keys, values = keyvals[:, :HEAD_DIM], keyvals[:, HEAD_DIM:]
    scores_ref[...] = lax.dot_general(
        stacked, keys, (((1,), (1,)), ((), ())), preferred_element_type=jnp.float32
    )
    denoms = []
    for h in range(heads):
        at = slice(h * half, (h + 1) * half)
        scores = scores_ref[at, :] * (scale_ref[h] * HEAD_DIM ** (-0.5))
        expon = jnp.exp(scores - jnp.max(scores, axis=1, keepdims=True))
        denoms.append(jnp.sum(expon, axis=1, keepdims=True))
        prob_ref[at, :] = expon.astype(jnp.bfloat16)
    context = jnp.dot(prob_ref[...], values, preferred_element_type=jnp.float32)
    context = jnp.concatenate(
        [
            (context[h * half : (h + 1) * half] / denoms[h]).astype(jnp.bfloat16)
            for h in [2 * zz + cc for cc in range(2) for zz in range(heads // 2)]
        ],
        axis=1,
    )
    remote(
        wout.at[other], wout.at[other], wc_send.at[1], wc_recv.at[1], sibling
    ).wait_recv()
    attended_ref[...] = jnp.dot(
        context,
        wout[...].reshape(heads * HEAD_DIM, attended_ref.shape[1]),
        preferred_element_type=jnp.float32,
    ).astype(jnp.bfloat16)

    for copy in started:
        copy.wait_send()
    for k in range(1, 4):
        b = 2 * flip(z, k) + c
        remote(
            win.at[b], win.at[b], act_send.at[3 + k], act_recv.at[b], sibling
        ).wait_send()


def fused(
    features, norm_gain, conv_weight, conv_bias, attn_gain,
    query_weight, keyval_weight, head_scale, output_weight,
):
    block, channels = features.shape
    half = block // 2
    taps, _, width = conv_weight.shape
    heads = head_scale.shape[0]
    total = 8 * width
    rows = 8 * block + 2 * EDGE
    qkv_cols = query_weight.shape[1] + keyval_weight.shape[1]
    f32, bf16 = jnp.float32, jnp.bfloat16
    dma = pltpu.SemaphoreType.DMA
    vmem = pl.BlockSpec(memory_space=pltpu.VMEM)
    smem = pl.BlockSpec(memory_space=pltpu.SMEM)
    coarse, attended = pl.pallas_call(
        fused_kernel,
        out_shape=(
            jax.ShapeDtypeStruct((8, half, width), bf16),
            jax.ShapeDtypeStruct((half, total), bf16),
        ),
        in_specs=[vmem, vmem, pl.BlockSpec(memory_space=pl.ANY)] + [vmem] * 4 + [smem, vmem],
        out_specs=(vmem, vmem),
        scratch_shapes=[
            pltpu.VMEM((8, block, channels), bf16),
            pltpu.VMEM((taps, 2 * block + 2 * MARGIN, 128), f32),
            pltpu.VMEM((taps, 2 * block + 2 * MARGIN, 128), f32),
            pltpu.VMEM((rows, 128), f32),
            pltpu.VMEM((rows, 128), f32),
            pltpu.VMEM((8, half, width), bf16),
            pltpu.VMEM((8, half, width), bf16),
            pltpu.VMEM((2, 4, query_weight.shape[0], qkv_cols), bf16),
            pltpu.VMEM((2, 4) + output_weight.shape, bf16),
            pltpu.VMEM((8, half, keyval_weight.shape[1]), bf16),
            pltpu.VMEM((8, 1, width), f32),
            pltpu.VMEM((8, 1, width), f32),
            pltpu.VMEM((taps, width, channels), bf16),
            pltpu.VMEM((heads * half, 8 * half), f32),
            pltpu.VMEM((heads * half, 8 * half), bf16),
            dma(()),
            dma((7,)), dma((8,)),
            dma((2, 4)), dma((2, 4)),
            dma((2, 4, 4)), dma((2, 4, 4)),
            dma((2,)), dma((2,)),
            dma((8,)), dma((8,)),
            dma((8,)), dma((8,)),
        ],
        compiler_params=pltpu.CompilerParams(
            collective_id=0, has_side_effects=True, vmem_limit_bytes=60 * 1024 * 1024
        ),
    )(
        features,
        norm_gain,
        conv_weight.transpose(0, 2, 1),
        conv_bias,
        attn_gain,
        query_weight,
        keyval_weight,
        head_scale,
        output_weight,
    )
    return coarse.transpose(1, 0, 2).reshape(half, total), attended


def normalize(values_in, channel_gain):
    meansq = jnp.mean(values_in * values_in, axis=-1, keepdims=True)
    return values_in * lax.rsqrt(meansq + 1e-06) * channel_gain


def convolve(padded, kernel, row_count):
    summed = jnp.zeros((row_count, kernel.shape[2]), jnp.float32)
    for kernel_tap in range(kernel.shape[0]):
        summed = summed + jnp.dot(
            padded[kernel_tap : kernel_tap + row_count],
            kernel[kernel_tap],
            preferred_element_type=jnp.float32,
        )
    return summed


def pool_pairs(levels):
    return jnp.max(levels.reshape(-1, 2, levels.shape[1]), axis=1)


def attend(queries, keyvals, scales):
    row_count = queries.shape[0]
    head_count = scales.shape[0]
    shaped = queries.reshape(row_count, head_count, HEAD_DIM)
    key_block = lax.all_gather(keyvals, "seq", axis=0, tiled=True)
    running_max = jnp.full((head_count, row_count), -1e30, jnp.float32)
    key_part = key_block[:, :HEAD_DIM]
    value_part = key_block[:, HEAD_DIM:]
    scores = (
        jnp.einsum("qhd,kd->hqk", shaped, key_part, preferred_element_type=jnp.float32)
        * scales[:, None, None]
        * HEAD_DIM ** (-0.5)
    )
    newest = jnp.maximum(running_max, jnp.max(scores, axis=2))
    expon = jnp.exp(scores - newest[:, :, None])
    running_sum = jnp.sum(expon, axis=2)
    running_ctx = jnp.einsum(
        "hqk,kd->hqd", expon.astype(jnp.bfloat16), value_part, preferred_element_type=jnp.float32
    )
    context = running_ctx / running_sum[:, :, None]
    return context.transpose(1, 0, 2).reshape(row_count, head_count * HEAD_DIM).astype(jnp.bfloat16)


def shards(
    features,
    norm_gain,
    conv_weight,
    conv_bias,
    attn_gain,
    query_weight,
    keyval_weight,
    head_scale,
    output_weight,
):
    normed = jax.nn.gelu(normalize(features.astype(jnp.float32), norm_gain)).astype(jnp.bfloat16)
    window = lax.all_gather(normed, "seq", axis=0, tiled=True)
    fine_rows = window.shape[0]
    width = conv_weight.shape[0] // 2
    padded = jnp.pad(window, ((width, width), (0, 0)))
    channels = conv_weight.shape[2]
    own_bias = lax.dynamic_slice_in_dim(conv_bias, lax.axis_index("seq") * channels, channels)
    levels = convolve(padded, conv_weight, fine_rows) + own_bias[None, :]
    pooled = pool_pairs(levels).astype(jnp.bfloat16)
    coarse = lax.all_to_all(pooled, "seq", split_axis=0, concat_axis=1, tiled=True)
    attn_in = normalize(coarse.astype(jnp.float32), attn_gain).astype(jnp.bfloat16)
    columns = attn_in
    query_sum = jnp.dot(
        columns,
        lax.all_gather(query_weight, "seq", axis=0, tiled=True),
        preferred_element_type=jnp.float32,
    )
    keyval_sum = jnp.dot(
        columns,
        lax.all_gather(keyval_weight, "seq", axis=0, tiled=True),
        preferred_element_type=jnp.float32,
    )
    queries = query_sum.astype(jnp.bfloat16)
    keyvals = keyval_sum.astype(jnp.bfloat16)
    context = attend(queries, keyvals, head_scale)
    columns = context
    projected = jnp.dot(
        columns,
        lax.all_gather(output_weight, "seq", axis=0, tiled=True),
        preferred_element_type=jnp.float32,
    )
    return (coarse, projected.astype(jnp.bfloat16))


def solution(mesh):
    fits = mesh.shape["dp"] == 4 and mesh.shape["seq"] == 8
    return jax.shard_map(
        fused if fits else shards,
        mesh=mesh,
        in_specs=(
            P(("dp", "seq"), None),
            P(),
            P(None, None, "seq"),
            P(),
            P(),
            P("seq", None),
            P("seq", None),
            P(),
            P("seq", None),
        ),
        out_specs=(P(("dp", "seq"), None), P(("dp", "seq"), None)),
        check_vma=False,
    )
```

```python
import jax
import jax.numpy as jnp
from jax import lax
from jax.experimental import pallas as pl
from jax.experimental.pallas import tpu as pltpu
from jax.sharding import PartitionSpec as P

HEAD_DIM = 128
MESH = pl.DeviceIdType.MESH
MARGIN = 16
EDGE = 8


def nearest(z, k):
    upper = lax.div(z, 2)
    if k == 0:
        return z
    if k == 1:
        return z + 1 - 2 * lax.rem(z, 2)
    return k - upper * (2 * k - 3)


def fused_kernel(
    feat_ref, ngain_ref, cw_ref, bias_ref, again_ref, wq_ref, wkv_ref, scale_ref, wo_ref,
    coarse_ref, attended_ref,
    win, tmp0, tmp1, acc0, acc1, csend, cbuf, wqkv, wout, kvbuf,
    bias8, again8, cw, cwt, scores_ref, prob_ref, cw_sem, act_send, act_recv, wa_send, wa_recv, wb_send, wb_recv, wc_send, wc_recv,
    co_send, co_recv, kv_send, kv_recv,
):
    p = lax.axis_index("dp")
    s = lax.axis_index("seq")
    z, c = lax.div(s, 2), lax.rem(s, 2)
    other = 1 - c
    sibling = (p, 2 * z + other)
    block = feat_ref.shape[0]
    half = block // 2
    heads = scale_ref.shape[0]
    qcols = wq_ref.shape[1]
    taps = cw_ref.shape[0]
    width = cw_ref.shape[1]
    depth = wq_ref.shape[0] // 4
    odepth = wo_ref.shape[0] // 4

    def remote(src, dst, send, recv, device):
        return pltpu.make_async_remote_copy(
            src_ref=src, dst_ref=dst, send_sem=send, recv_sem=recv,
            device_id=device, device_id_type=MESH,
        )

    load = pltpu.make_async_copy(cw_ref, cw, cw_sem)
    load.start()
    barrier = pltpu.get_barrier_semaphore()
    for k in range(1, 8):
        pl.semaphore_signal(
            barrier, inc=1, device_id=(p, lax.rem(s + k, 8)), device_id_type=MESH
        )
    for k in range(1, 4):
        pl.semaphore_signal(
            barrier, inc=1, device_id=(lax.rem(p + k, 4), s), device_id_type=MESH
        )
    wqkv[c, z, :, :qcols] = wq_ref[...]
    wqkv[c, z, :, qcols:] = wkv_ref[...]
    wout[c, z] = wo_ref[...]
    pl.semaphore_wait(barrier, 10)

    started = []

    def qkv_part(cc, zz, pp):
        return wqkv.at[cc, zz, pl.ds(pl.multiple_of(pp * depth, 16), depth), :]

    def out_part(cc, zz, pp):
        return wout.at[cc, zz, pl.ds(pl.multiple_of(pp * odepth, 16), odepth), :]

    parts = (qkv_part, out_part)

    def along_z(n):
        here = parts[n](c, z, p)
        for k in range(1, 4):
            copy = remote(
                here, here, wa_send.at[n, k], wa_recv.at[n, z], (p, 2 * nearest(z, k) + c)
            )
            copy.start()
            started.append(copy)

    def along_dp(n):
        for k in range(1, 4):
            zz = nearest(z, k)
            here = parts[n](c, zz, p)
            remote(here, here, wa_send.at[n, 0], wa_recv.at[n, zz], sibling).wait_recv()
            for m in range(1, 4):
                copy = remote(
                    here, here, wb_send.at[n, k, m], wb_recv.at[n, zz, p],
                    (lax.rem(p + m, 4), s),
                )
                copy.start()
                started.append(copy)

    def along_core(n):
        for k in range(1, 4):
            zz = nearest(z, k)
            for m in range(1, 4):
                pp = lax.rem(p + m, 4)
                there = parts[n](c, zz, pp)
                remote(
                    there, there, wa_send.at[n, 0], wb_recv.at[n, zz, pp], sibling
                ).wait_recv()
        half_of = (wqkv, wout)[n].at[c]
        copy = remote(half_of, half_of, wc_send.at[n], wc_recv.at[n], sibling)
        copy.start()
        started.append(copy)

    along_z(0)

    x = feat_ref[...].astype(jnp.float32)
    meansq = jnp.mean(x * x, axis=-1, keepdims=True)
    normed = x * lax.rsqrt(meansq + 1e-06) * ngain_ref[...][None, :]
    win[s] = jax.nn.gelu(normed).astype(jnp.bfloat16)
    for k in range(1, 4):
        copy = remote(
            win.at[s], win.at[s], act_send.at[k], act_recv.at[s], (p, 2 * nearest(z, k) + c)
        )
        copy.start()
        started.append(copy)
    copy = remote(win.at[s], win.at[s], act_send.at[0], act_recv.at[s], sibling)
    copy.start()
    started.append(copy)

    acc0[...] = jnp.zeros_like(acc0)
    acc1[...] = jnp.zeros_like(acc1)
    tmp0[...] = jnp.zeros_like(tmp0)
    tmp1[...] = jnp.zeros_like(tmp1)

    def convolve_pair(zz):
        rows = win[pl.ds(2 * zz, 2)].reshape(2 * block, win.shape[2])
        for t in range(taps):
            y = jnp.dot(rows, cwt[t], preferred_element_type=jnp.float32)
            tmp0[t, MARGIN : MARGIN + 2 * block, :] = y[:, :128]
            tmp1[t, MARGIN : MARGIN + 2 * block, : width - 128] = y[:, 128:]
        span = 2 * block + 2 * EDGE
        first = MARGIN - EDGE - taps // 2
        at = pl.ds(pl.multiple_of(zz * 2 * block, 8), span)
        for tmp, acc in ((tmp0, acc0), (tmp1, acc1)):
            total = tmp[0, first : first + span, :]
            for t in range(1, taps):
                total = total + tmp[t, first + t : first + t + span, :]
            acc[at, :] += total

    def wait_block(b):
        remote(win.at[b], win.at[b], act_send.at[0], act_recv.at[b], sibling).wait_recv()

    load.wait()
    for t in range(taps):
        cwt[t] = cw[t].T
    bias_row, again_row = bias_ref[...][None, :], again_ref[...][None, :]
    for j in range(8):
        bias8[j] = bias_row[:, j * width : (j + 1) * width]
        again8[j] = again_row[:, j * width : (j + 1) * width]

    def step(k):
        zz = nearest(z, k)
        if k > 0:
            b = 2 * zz + c
            wait_block(b)
            copy = remote(
                win.at[b], win.at[b], act_send.at[3 + k], act_recv.at[b], sibling
            )
            copy.start()
            started.append(copy)
        wait_block(2 * zz + other)
        convolve_pair(zz)

    def pooled(r, out):
        start = pl.multiple_of(r * block, 8) + EDGE
        bias = bias8[s]
        c0 = jnp.maximum(
            acc0[pl.ds(start, half, stride=2), :], acc0[pl.ds(start + 1, half, stride=2), :]
        )
        c1 = jnp.maximum(
            acc1[pl.ds(start, half, stride=2), :], acc1[pl.ds(start + 1, half, stride=2), :]
        )
        c1 = (c1[:, : width - 128] + bias[:, 128:]).astype(jnp.bfloat16)
        out[:half, :] = (c0 + bias[:, :128]).astype(jnp.bfloat16)
        out[half:, :64] = c1[: half // 2]
        out[half:, 64:] = c1[half // 2 :]

    def send_rows(k, r):
        pooled(r, csend.at[r])
        copy = remote(csend.at[r], cbuf.at[s], co_send.at[k], co_recv.at[s], (p, r))
        copy.start()
        started.append(copy)

    step(0)
    along_dp(0)
    step(1)
    along_z(1)
    step(2)
    upper = lax.div(z, 2)
    send_rows(4, 4 - upper)
    for k in range(1, 4):
        send_rows(k, 4 * upper + lax.rem(s + k, 4))
    pooled(s, cbuf.at[s])
    along_core(0)
    step(3)
    for k in range(5, 8):
        send_rows(k, k + upper * (7 - 2 * k))
    along_dp(1)
    for k in range(1, 8):
        r = lax.rem(s + k, 8)
        remote(csend.at[r], cbuf.at[r], co_send.at[0], co_recv.at[r], sibling).wait_recv()

    squares = jnp.zeros((half, 1), jnp.float32)
    pieces = []
    for j in range(8):
        narrow = jnp.concatenate([cbuf[j, half:, :64], cbuf[j, half:, 64:]], axis=0)
        piece = jnp.concatenate([cbuf[j, :half, :], narrow], axis=1)
        pieces.append(piece)
        piece = piece.astype(jnp.float32)
        squares = squares + jnp.sum(piece * piece, axis=-1, keepdims=True)
    inverse = lax.rsqrt(squares / (8 * width) + 1e-06)

    remote(
        wqkv.at[other], wqkv.at[other], wc_send.at[0], wc_recv.at[0], sibling
    ).wait_recv()
    attn = []
    kv = jnp.zeros((half, wkv_ref.shape[1]), jnp.float32)
    for j in range(8):
        piece = (pieces[j].astype(jnp.float32) * inverse * again8[j]).astype(jnp.bfloat16)
        attn.append(piece)
        kv = kv + jnp.dot(
            piece, wqkv[j % 2, j // 2, :, qcols:], preferred_element_type=jnp.float32
        )
    kvbuf[s] = kv.astype(jnp.bfloat16)
    for k in range(1, 4):
        copy = remote(
            kvbuf.at[s], kvbuf.at[s], kv_send.at[k], kv_recv.at[s], (p, 2 * nearest(z, k) + c)
        )
        copy.start()
        started.append(copy)
    copy = remote(kvbuf.at[s], kvbuf.at[s], kv_send.at[0], kv_recv.at[s], sibling)
    copy.start()
    started.append(copy)
    for j in range(8):
        coarse_ref[:, j * width : (j + 1) * width] = pieces[j]
    query = jnp.zeros((half, qcols), jnp.float32)
    for j in range(8):
        query = query + jnp.dot(
            attn[j], wqkv[j % 2, j // 2, :, :qcols], preferred_element_type=jnp.float32
        )
    query = query.astype(jnp.bfloat16)
    stacked = jnp.concatenate(
        [query[:, h * HEAD_DIM : (h + 1) * HEAD_DIM] for h in range(heads)], axis=0
    )
    for k in range(1, 4):
        b = 2 * nearest(z, k) + c
        remote(kvbuf.at[b], kvbuf.at[b], kv_send.at[0], kv_recv.at[b], sibling).wait_recv()
        copy = remote(kvbuf.at[b], kvbuf.at[b], kv_send.at[3 + k], kv_recv.at[b], sibling)
        copy.start()
        started.append(copy)
    along_core(1)
    for k in range(4):
        b = 2 * nearest(z, k) + other
        remote(kvbuf.at[b], kvbuf.at[b], kv_send.at[0], kv_recv.at[b], sibling).wait_recv()

    keyvals = kvbuf[...].reshape(8 * half, kvbuf.shape[2])
    keys, values = keyvals[:, :HEAD_DIM], keyvals[:, HEAD_DIM:]
    scores_ref[...] = lax.dot_general(
        stacked, keys, (((1,), (1,)), ((), ())), preferred_element_type=jnp.float32
    )
    denoms = []
    for h in range(heads):
        at = slice(h * half, (h + 1) * half)
        scores = scores_ref[at, :] * (scale_ref[h] * HEAD_DIM ** (-0.5))
        expon = jnp.exp(scores - jnp.max(scores, axis=1, keepdims=True))
        denoms.append(jnp.sum(expon, axis=1, keepdims=True))
        prob_ref[at, :] = expon.astype(jnp.bfloat16)
    context = jnp.dot(prob_ref[...], values, preferred_element_type=jnp.float32)
    context = jnp.concatenate(
        [
            (context[h * half : (h + 1) * half] / denoms[h]).astype(jnp.bfloat16)
            for h in [2 * zz + cc for cc in range(2) for zz in range(heads // 2)]
        ],
        axis=1,
    )
    remote(
        wout.at[other], wout.at[other], wc_send.at[1], wc_recv.at[1], sibling
    ).wait_recv()
    attended_ref[...] = jnp.dot(
        context,
        wout[...].reshape(heads * HEAD_DIM, attended_ref.shape[1]),
        preferred_element_type=jnp.float32,
    ).astype(jnp.bfloat16)

    for copy in started:
        copy.wait_send()


def fused(
    features, norm_gain, conv_weight, conv_bias, attn_gain,
    query_weight, keyval_weight, head_scale, output_weight,
):
    block, channels = features.shape
    half = block // 2
    taps, _, width = conv_weight.shape
    heads = head_scale.shape[0]
    total = 8 * width
    rows = 8 * block + 2 * EDGE
    qkv_cols = query_weight.shape[1] + keyval_weight.shape[1]
    f32, bf16 = jnp.float32, jnp.bfloat16
    dma = pltpu.SemaphoreType.DMA
    vmem = pl.BlockSpec(memory_space=pltpu.VMEM)
    smem = pl.BlockSpec(memory_space=pltpu.SMEM)
    coarse, attended = pl.pallas_call(
        fused_kernel,
        out_shape=(
            jax.ShapeDtypeStruct((half, total), bf16),
            jax.ShapeDtypeStruct((half, total), bf16),
        ),
        in_specs=[vmem, vmem, pl.BlockSpec(memory_space=pl.ANY)] + [vmem] * 4 + [smem, vmem],
        out_specs=(vmem, vmem),
        scratch_shapes=[
            pltpu.VMEM((8, block, channels), bf16),
            pltpu.VMEM((taps, 2 * block + 2 * MARGIN, 128), f32),
            pltpu.VMEM((taps, 2 * block + 2 * MARGIN, 128), f32),
            pltpu.VMEM((rows, 128), f32),
            pltpu.VMEM((rows, 128), f32),
            pltpu.VMEM((8, half + half // 2, 128), bf16),
            pltpu.VMEM((8, half + half // 2, 128), bf16),
            pltpu.VMEM((2, 4, query_weight.shape[0], qkv_cols), bf16),
            pltpu.VMEM((2, 4) + output_weight.shape, bf16),
            pltpu.VMEM((8, half, keyval_weight.shape[1]), bf16),
            pltpu.VMEM((8, 1, width), f32),
            pltpu.VMEM((8, 1, width), f32),
            pltpu.VMEM((taps, width, channels), bf16),
            pltpu.VMEM((taps, channels, width), bf16),
            pltpu.VMEM((heads * half, 8 * half), f32),
            pltpu.VMEM((heads * half, 8 * half), bf16),
            dma(()),
            dma((7,)), dma((8,)),
            dma((2, 4)), dma((2, 4)),
            dma((2, 4, 4)), dma((2, 4, 4)),
            dma((2,)), dma((2,)),
            dma((8,)), dma((8,)),
            dma((8,)), dma((8,)),
        ],
        compiler_params=pltpu.CompilerParams(
            collective_id=0, has_side_effects=True, vmem_limit_bytes=60 * 1024 * 1024
        ),
    )(
        features,
        norm_gain,
        conv_weight.transpose(0, 2, 1),
        conv_bias,
        attn_gain,
        query_weight,
        keyval_weight,
        head_scale,
        output_weight,
    )
    return coarse, attended


def normalize(values_in, channel_gain):
    meansq = jnp.mean(values_in * values_in, axis=-1, keepdims=True)
    return values_in * lax.rsqrt(meansq + 1e-06) * channel_gain


def convolve(padded, kernel, row_count):
    summed = jnp.zeros((row_count, kernel.shape[2]), jnp.float32)
    for kernel_tap in range(kernel.shape[0]):
        summed = summed + jnp.dot(
            padded[kernel_tap : kernel_tap + row_count],
            kernel[kernel_tap],
            preferred_element_type=jnp.float32,
        )
    return summed


def pool_pairs(levels):
    return jnp.max(levels.reshape(-1, 2, levels.shape[1]), axis=1)


def attend(queries, keyvals, scales):
    row_count = queries.shape[0]
    head_count = scales.shape[0]
    shaped = queries.reshape(row_count, head_count, HEAD_DIM)
    key_block = lax.all_gather(keyvals, "seq", axis=0, tiled=True)
    running_max = jnp.full((head_count, row_count), -1e30, jnp.float32)
    key_part = key_block[:, :HEAD_DIM]
    value_part = key_block[:, HEAD_DIM:]
    scores = (
        jnp.einsum("qhd,kd->hqk", shaped, key_part, preferred_element_type=jnp.float32)
        * scales[:, None, None]
        * HEAD_DIM ** (-0.5)
    )
    newest = jnp.maximum(running_max, jnp.max(scores, axis=2))
    expon = jnp.exp(scores - newest[:, :, None])
    running_sum = jnp.sum(expon, axis=2)
    running_ctx = jnp.einsum(
        "hqk,kd->hqd", expon.astype(jnp.bfloat16), value_part, preferred_element_type=jnp.float32
    )
    context = running_ctx / running_sum[:, :, None]
    return context.transpose(1, 0, 2).reshape(row_count, head_count * HEAD_DIM).astype(jnp.bfloat16)


def shards(
    features,
    norm_gain,
    conv_weight,
    conv_bias,
    attn_gain,
    query_weight,
    keyval_weight,
    head_scale,
    output_weight,
):
    normed = jax.nn.gelu(normalize(features.astype(jnp.float32), norm_gain)).astype(jnp.bfloat16)
    window = lax.all_gather(normed, "seq", axis=0, tiled=True)
    fine_rows = window.shape[0]
    width = conv_weight.shape[0] // 2
    padded = jnp.pad(window, ((width, width), (0, 0)))
    channels = conv_weight.shape[2]
    own_bias = lax.dynamic_slice_in_dim(conv_bias, lax.axis_index("seq") * channels, channels)
    levels = convolve(padded, conv_weight, fine_rows) + own_bias[None, :]
    pooled = pool_pairs(levels).astype(jnp.bfloat16)
    coarse = lax.all_to_all(pooled, "seq", split_axis=0, concat_axis=1, tiled=True)
    attn_in = normalize(coarse.astype(jnp.float32), attn_gain).astype(jnp.bfloat16)
    columns = attn_in
    query_sum = jnp.dot(
        columns,
        lax.all_gather(query_weight, "seq", axis=0, tiled=True),
        preferred_element_type=jnp.float32,
    )
    keyval_sum = jnp.dot(
        columns,
        lax.all_gather(keyval_weight, "seq", axis=0, tiled=True),
        preferred_element_type=jnp.float32,
    )
    queries = query_sum.astype(jnp.bfloat16)
    keyvals = keyval_sum.astype(jnp.bfloat16)
    context = attend(queries, keyvals, head_scale)
    columns = context
    projected = jnp.dot(
        columns,
        lax.all_gather(output_weight, "seq", axis=0, tiled=True),
        preferred_element_type=jnp.float32,
    )
    return (coarse, projected.astype(jnp.bfloat16))


def solution(mesh):
    fits = mesh.shape["dp"] == 4 and mesh.shape["seq"] == 8
    return jax.shard_map(
        fused if fits else shards,
        mesh=mesh,
        in_specs=(
            P(("dp", "seq"), None),
            P(),
            P(None, None, "seq"),
            P(),
            P(),
            P("seq", None),
            P("seq", None),
            P(),
            P("seq", None),
        ),
        out_specs=(P(("dp", "seq"), None), P(("dp", "seq"), None)),
        check_vma=False,
    )
```

```python
import jax
import jax.numpy as jnp
from jax import lax
from jax.experimental import pallas as pl
from jax.experimental.pallas import tpu as pltpu
from jax.sharding import PartitionSpec as P

HEAD_DIM = 128
MESH = pl.DeviceIdType.MESH
MARGIN = 16
EDGE = 8


def nearest(z, k):
    upper = lax.div(z, 2)
    if k == 0:
        return z
    if k == 1:
        return z + 1 - 2 * lax.rem(z, 2)
    return k - upper * (2 * k - 3)


def fused_kernel(
    feat_ref, ngain_ref, cw_ref, bias_ref, again_ref, wq_ref, wkv_ref, scale_ref, wo_ref,
    coarse_ref, attended_ref,
    win, tmp0, tmp1, acc0, acc1, csend, cbuf, wqkv, wout, kvbuf,
    bias8, again8, cw, cwt, scores_ref, prob_ref, cw_sem, act_send, act_recv, wa_send, wa_recv, wb_send, wb_recv, wc_send, wc_recv,
    co_send, co_recv, kv_send, kv_recv,
):
    p = lax.axis_index("dp")
    s = lax.axis_index("seq")
    z, c = lax.div(s, 2), lax.rem(s, 2)
    other = 1 - c
    sibling = (p, 2 * z + other)
    block = feat_ref.shape[0]
    half = block // 2
    heads = scale_ref.shape[0]
    qcols = wq_ref.shape[1]
    taps = cw_ref.shape[0]
    width = cw_ref.shape[1]
    depth = wq_ref.shape[0] // 4
    odepth = wo_ref.shape[0] // 4

    def remote(src, dst, send, recv, device):
        return pltpu.make_async_remote_copy(
            src_ref=src, dst_ref=dst, send_sem=send, recv_sem=recv,
            device_id=device, device_id_type=MESH,
        )

    load = pltpu.make_async_copy(cw_ref, cw, cw_sem)
    load.start()
    barrier = pltpu.get_barrier_semaphore()
    for k in range(1, 8):
        pl.semaphore_signal(
            barrier, inc=1, device_id=(p, lax.rem(s + k, 8)), device_id_type=MESH
        )
    for k in range(1, 4):
        pl.semaphore_signal(
            barrier, inc=1, device_id=(lax.rem(p + k, 4), s), device_id_type=MESH
        )
    wqkv[c, z, :, :qcols] = wq_ref[...]
    wqkv[c, z, :, qcols:] = wkv_ref[...]
    wout[c, z] = wo_ref[...]
    pl.semaphore_wait(barrier, 10)

    started = []

    def qkv_part(cc, zz, pp):
        return wqkv.at[cc, zz, pl.ds(pl.multiple_of(pp * depth, 16), depth), :]

    def out_part(cc, zz, pp):
        return wout.at[cc, zz, pl.ds(pl.multiple_of(pp * odepth, 16), odepth), :]

    parts = (qkv_part, out_part)
    middle = lax.rem(lax.div(z + 1, 2), 2) == 1
    end = (p, 2 * nearest(z, 1) + c)
    relays = []

    def relay(ref, send, recv):
        copy = remote(ref, ref, send, recv, end)
        relays.append(copy)

        @pl.when(middle)
        def _():
            copy.start()

    def along_z(n):
        here = parts[n](c, z, p)
        for k in range(1, 3):
            copy = remote(
                here, here, wa_send.at[n, k], wa_recv.at[n, z], (p, 2 * nearest(z, k) + c)
            )
            copy.start()
            started.append(copy)

    def along_dp(n):
        for k in range(1, 4):
            zz = nearest(z, k)
            here = parts[n](c, zz, p)
            remote(here, here, wa_send.at[n, 0], wa_recv.at[n, zz], sibling).wait_recv()
            if k > 1:
                relay(here, wa_send.at[n, 1 + k], wa_recv.at[n, zz])
            for m in range(1, 4):
                copy = remote(
                    here, here, wb_send.at[n, k, m], wb_recv.at[n, zz, p],
                    (lax.rem(p + m, 4), s),
                )
                copy.start()
                started.append(copy)

    def along_core(n):
        for k in range(1, 4):
            zz = nearest(z, k)
            for m in range(1, 4):
                pp = lax.rem(p + m, 4)
                there = parts[n](c, zz, pp)
                remote(
                    there, there, wa_send.at[n, 0], wb_recv.at[n, zz, pp], sibling
                ).wait_recv()
        half_of = (wqkv, wout)[n].at[c]
        copy = remote(half_of, half_of, wc_send.at[n], wc_recv.at[n], sibling)
        copy.start()
        started.append(copy)

    along_z(0)

    x = feat_ref[...].astype(jnp.float32)
    meansq = jnp.mean(x * x, axis=-1, keepdims=True)
    normed = x * lax.rsqrt(meansq + 1e-06) * ngain_ref[...][None, :]
    win[s] = jax.nn.gelu(normed).astype(jnp.bfloat16)
    for k in range(1, 3):
        copy = remote(
            win.at[s], win.at[s], act_send.at[k], act_recv.at[s], (p, 2 * nearest(z, k) + c)
        )
        copy.start()
        started.append(copy)
    copy = remote(win.at[s], win.at[s], act_send.at[0], act_recv.at[s], sibling)
    copy.start()
    started.append(copy)

    acc0[...] = jnp.zeros_like(acc0)
    acc1[...] = jnp.zeros_like(acc1)
    tmp0[...] = jnp.zeros_like(tmp0)
    tmp1[...] = jnp.zeros_like(tmp1)

    def convolve_pair(zz):
        rows = win[pl.ds(2 * zz, 2)].reshape(2 * block, win.shape[2])
        for t in range(taps):
            y = jnp.dot(rows, cwt[t], preferred_element_type=jnp.float32)
            tmp0[t, MARGIN : MARGIN + 2 * block, :] = y[:, :128]
            tmp1[t, MARGIN : MARGIN + 2 * block, : width - 128] = y[:, 128:]
        span = 2 * block + 2 * EDGE
        first = MARGIN - EDGE - taps // 2
        at = pl.ds(pl.multiple_of(zz * 2 * block, 8), span)
        for tmp, acc in ((tmp0, acc0), (tmp1, acc1)):
            total = tmp[0, first : first + span, :]
            for t in range(1, taps):
                total = total + tmp[t, first + t : first + t + span, :]
            acc[at, :] += total

    def wait_block(b):
        remote(win.at[b], win.at[b], act_send.at[0], act_recv.at[b], sibling).wait_recv()

    load.wait()
    for t in range(taps):
        cwt[t] = cw[t].T
    bias_row, again_row = bias_ref[...][None, :], again_ref[...][None, :]
    for j in range(8):
        bias8[j] = bias_row[:, j * width : (j + 1) * width]
        again8[j] = again_row[:, j * width : (j + 1) * width]

    def step(k):
        zz = nearest(z, k)
        if k > 0:
            b = 2 * zz + c
            wait_block(b)
            copy = remote(
                win.at[b], win.at[b], act_send.at[3 + k], act_recv.at[b], sibling
            )
            if k > 1:
                relay(win.at[b], act_send.at[5 + k], act_recv.at[b])
            copy.start()
            started.append(copy)
        if k == 3:
            along_dp(1)
        wait_block(2 * zz + other)
        convolve_pair(zz)

    def pooled(r, out):
        start = pl.multiple_of(r * block, 8) + EDGE
        bias = bias8[s]
        c0 = jnp.maximum(
            acc0[pl.ds(start, half, stride=2), :], acc0[pl.ds(start + 1, half, stride=2), :]
        )
        c1 = jnp.maximum(
            acc1[pl.ds(start, half, stride=2), :], acc1[pl.ds(start + 1, half, stride=2), :]
        )
        c1 = (c1[:, : width - 128] + bias[:, 128:]).astype(jnp.bfloat16)
        out[:half, :] = (c0 + bias[:, :128]).astype(jnp.bfloat16)
        out[half:, :64] = c1[: half // 2]
        out[half:, 64:] = c1[half // 2 :]

    def send_rows(k, r):
        pooled(r, csend.at[r])
        copy = remote(csend.at[r], cbuf.at[s], co_send.at[k], co_recv.at[s], (p, r))
        copy.start()
        started.append(copy)

    step(0)
    along_dp(0)
    step(1)
    along_z(1)
    step(2)
    upper = lax.div(z, 2)
    send_rows(4, 4 - upper)
    for k in range(1, 4):
        send_rows(k, 4 * upper + lax.rem(s + k, 4))
    pooled(s, cbuf.at[s])
    along_core(0)
    step(3)
    for k in range(5, 8):
        send_rows(k, k + upper * (7 - 2 * k))
    for k in range(1, 8):
        r = lax.rem(s + k, 8)
        remote(csend.at[r], cbuf.at[r], co_send.at[0], co_recv.at[r], sibling).wait_recv()

    squares = jnp.zeros((half, 1), jnp.float32)
    pieces = []
    for j in range(8):
        narrow = jnp.concatenate([cbuf[j, half:, :64], cbuf[j, half:, 64:]], axis=0)
        piece = jnp.concatenate([cbuf[j, :half, :], narrow], axis=1)
        pieces.append(piece)
        piece = piece.astype(jnp.float32)
        squares = squares + jnp.sum(piece * piece, axis=-1, keepdims=True)
    inverse = lax.rsqrt(squares / (8 * width) + 1e-06)

    remote(
        wqkv.at[other], wqkv.at[other], wc_send.at[0], wc_recv.at[0], sibling
    ).wait_recv()
    attn = []
    kv = jnp.zeros((half, wkv_ref.shape[1]), jnp.float32)
    for j in range(8):
        piece = (pieces[j].astype(jnp.float32) * inverse * again8[j]).astype(jnp.bfloat16)
        attn.append(piece)
        kv = kv + jnp.dot(
            piece, wqkv[j % 2, j // 2, :, qcols:], preferred_element_type=jnp.float32
        )
    kvbuf[s] = kv.astype(jnp.bfloat16)
    for k in range(1, 4):
        copy = remote(
            kvbuf.at[s], kvbuf.at[s], kv_send.at[k], kv_recv.at[s], (p, 2 * nearest(z, k) + c)
        )
        copy.start()
        started.append(copy)
    copy = remote(kvbuf.at[s], kvbuf.at[s], kv_send.at[0], kv_recv.at[s], sibling)
    copy.start()
    started.append(copy)
    for j in range(8):
        coarse_ref[:, j * width : (j + 1) * width] = pieces[j]
    query = jnp.zeros((half, qcols), jnp.float32)
    for j in range(8):
        query = query + jnp.dot(
            attn[j], wqkv[j % 2, j // 2, :, :qcols], preferred_element_type=jnp.float32
        )
    query = query.astype(jnp.bfloat16)
    stacked = jnp.concatenate(
        [query[:, h * HEAD_DIM : (h + 1) * HEAD_DIM] for h in range(heads)], axis=0
    )
    for k in range(1, 4):
        b = 2 * nearest(z, k) + c
        remote(kvbuf.at[b], kvbuf.at[b], kv_send.at[0], kv_recv.at[b], sibling).wait_recv()
        copy = remote(kvbuf.at[b], kvbuf.at[b], kv_send.at[3 + k], kv_recv.at[b], sibling)
        copy.start()
        started.append(copy)
    along_core(1)
    for k in range(4):
        b = 2 * nearest(z, k) + other
        remote(kvbuf.at[b], kvbuf.at[b], kv_send.at[0], kv_recv.at[b], sibling).wait_recv()

    keyvals = kvbuf[...].reshape(8 * half, kvbuf.shape[2])
    keys, values = keyvals[:, :HEAD_DIM], keyvals[:, HEAD_DIM:]
    scores_ref[...] = lax.dot_general(
        stacked, keys, (((1,), (1,)), ((), ())), preferred_element_type=jnp.float32
    )
    denoms = []
    for h in range(heads):
        at = slice(h * half, (h + 1) * half)
        scores = scores_ref[at, :] * (scale_ref[h] * HEAD_DIM ** (-0.5))
        expon = jnp.exp(scores - jnp.max(scores, axis=1, keepdims=True))
        denoms.append(jnp.sum(expon, axis=1, keepdims=True))
        prob_ref[at, :] = expon.astype(jnp.bfloat16)
    context = jnp.dot(prob_ref[...], values, preferred_element_type=jnp.float32)
    context = jnp.concatenate(
        [
            (context[h * half : (h + 1) * half] / denoms[h]).astype(jnp.bfloat16)
            for h in [2 * zz + cc for cc in range(2) for zz in range(heads // 2)]
        ],
        axis=1,
    )
    remote(
        wout.at[other], wout.at[other], wc_send.at[1], wc_recv.at[1], sibling
    ).wait_recv()
    attended_ref[...] = jnp.dot(
        context,
        wout[...].reshape(heads * HEAD_DIM, attended_ref.shape[1]),
        preferred_element_type=jnp.float32,
    ).astype(jnp.bfloat16)

    for copy in started:
        copy.wait_send()

    @pl.when(middle)
    def _():
        for copy in relays:
            copy.wait_send()


def fused(
    features, norm_gain, conv_weight, conv_bias, attn_gain,
    query_weight, keyval_weight, head_scale, output_weight,
):
    block, channels = features.shape
    half = block // 2
    taps, _, width = conv_weight.shape
    heads = head_scale.shape[0]
    total = 8 * width
    rows = 8 * block + 2 * EDGE
    qkv_cols = query_weight.shape[1] + keyval_weight.shape[1]
    f32, bf16 = jnp.float32, jnp.bfloat16
    dma = pltpu.SemaphoreType.DMA
    vmem = pl.BlockSpec(memory_space=pltpu.VMEM)
    smem = pl.BlockSpec(memory_space=pltpu.SMEM)
    coarse, attended = pl.pallas_call(
        fused_kernel,
        out_shape=(
            jax.ShapeDtypeStruct((half, total), bf16),
            jax.ShapeDtypeStruct((half, total), bf16),
        ),
        in_specs=[vmem, vmem, pl.BlockSpec(memory_space=pl.ANY)] + [vmem] * 4 + [smem, vmem],
        out_specs=(vmem, vmem),
        scratch_shapes=[
            pltpu.VMEM((8, block, channels), bf16),
            pltpu.VMEM((taps, 2 * block + 2 * MARGIN, 128), f32),
            pltpu.VMEM((taps, 2 * block + 2 * MARGIN, 128), f32),
            pltpu.VMEM((rows, 128), f32),
            pltpu.VMEM((rows, 128), f32),
            pltpu.VMEM((8, half + half // 2, 128), bf16),
            pltpu.VMEM((8, half + half // 2, 128), bf16),
            pltpu.VMEM((2, 4, query_weight.shape[0], qkv_cols), bf16),
            pltpu.VMEM((2, 4) + output_weight.shape, bf16),
            pltpu.VMEM((8, half, keyval_weight.shape[1]), bf16),
            pltpu.VMEM((8, 1, width), f32),
            pltpu.VMEM((8, 1, width), f32),
            pltpu.VMEM((taps, width, channels), bf16),
            pltpu.VMEM((taps, channels, width), bf16),
            pltpu.VMEM((heads * half, 8 * half), f32),
            pltpu.VMEM((heads * half, 8 * half), bf16),
            dma(()),
            dma((9,)), dma((8,)),
            dma((2, 5)), dma((2, 4)),
            dma((2, 4, 4)), dma((2, 4, 4)),
            dma((2,)), dma((2,)),
            dma((8,)), dma((8,)),
            dma((8,)), dma((8,)),
        ],
        compiler_params=pltpu.CompilerParams(
            collective_id=0, has_side_effects=True, vmem_limit_bytes=60 * 1024 * 1024
        ),
    )(
        features,
        norm_gain,
        conv_weight.transpose(0, 2, 1),
        conv_bias,
        attn_gain,
        query_weight,
        keyval_weight,
        head_scale,
        output_weight,
    )
    return coarse, attended


def normalize(values_in, channel_gain):
    meansq = jnp.mean(values_in * values_in, axis=-1, keepdims=True)
    return values_in * lax.rsqrt(meansq + 1e-06) * channel_gain


def convolve(padded, kernel, row_count):
    summed = jnp.zeros((row_count, kernel.shape[2]), jnp.float32)
    for kernel_tap in range(kernel.shape[0]):
        summed = summed + jnp.dot(
            padded[kernel_tap : kernel_tap + row_count],
            kernel[kernel_tap],
            preferred_element_type=jnp.float32,
        )
    return summed


def pool_pairs(levels):
    return jnp.max(levels.reshape(-1, 2, levels.shape[1]), axis=1)


def attend(queries, keyvals, scales):
    row_count = queries.shape[0]
    head_count = scales.shape[0]
    shaped = queries.reshape(row_count, head_count, HEAD_DIM)
    key_block = lax.all_gather(keyvals, "seq", axis=0, tiled=True)
    running_max = jnp.full((head_count, row_count), -1e30, jnp.float32)
    key_part = key_block[:, :HEAD_DIM]
    value_part = key_block[:, HEAD_DIM:]
    scores = (
        jnp.einsum("qhd,kd->hqk", shaped, key_part, preferred_element_type=jnp.float32)
        * scales[:, None, None]
        * HEAD_DIM ** (-0.5)
    )
    newest = jnp.maximum(running_max, jnp.max(scores, axis=2))
    expon = jnp.exp(scores - newest[:, :, None])
    running_sum = jnp.sum(expon, axis=2)
    running_ctx = jnp.einsum(
        "hqk,kd->hqd", expon.astype(jnp.bfloat16), value_part, preferred_element_type=jnp.float32
    )
    context = running_ctx / running_sum[:, :, None]
    return context.transpose(1, 0, 2).reshape(row_count, head_count * HEAD_DIM).astype(jnp.bfloat16)


def shards(
    features,
    norm_gain,
    conv_weight,
    conv_bias,
    attn_gain,
    query_weight,
    keyval_weight,
    head_scale,
    output_weight,
):
    normed = jax.nn.gelu(normalize(features.astype(jnp.float32), norm_gain)).astype(jnp.bfloat16)
    window = lax.all_gather(normed, "seq", axis=0, tiled=True)
    fine_rows = window.shape[0]
    width = conv_weight.shape[0] // 2
    padded = jnp.pad(window, ((width, width), (0, 0)))
    channels = conv_weight.shape[2]
    own_bias = lax.dynamic_slice_in_dim(conv_bias, lax.axis_index("seq") * channels, channels)
    levels = convolve(padded, conv_weight, fine_rows) + own_bias[None, :]
    pooled = pool_pairs(levels).astype(jnp.bfloat16)
    coarse = lax.all_to_all(pooled, "seq", split_axis=0, concat_axis=1, tiled=True)
    attn_in = normalize(coarse.astype(jnp.float32), attn_gain).astype(jnp.bfloat16)
    columns = attn_in
    query_sum = jnp.dot(
        columns,
        lax.all_gather(query_weight, "seq", axis=0, tiled=True),
        preferred_element_type=jnp.float32,
    )
    keyval_sum = jnp.dot(
        columns,
        lax.all_gather(keyval_weight, "seq", axis=0, tiled=True),
        preferred_element_type=jnp.float32,
    )
    queries = query_sum.astype(jnp.bfloat16)
    keyvals = keyval_sum.astype(jnp.bfloat16)
    context = attend(queries, keyvals, head_scale)
    columns = context
    projected = jnp.dot(
        columns,
        lax.all_gather(output_weight, "seq", axis=0, tiled=True),
        preferred_element_type=jnp.float32,
    )
    return (coarse, projected.astype(jnp.bfloat16))


def solution(mesh):
    fits = mesh.shape["dp"] == 4 and mesh.shape["seq"] == 8
    return jax.shard_map(
        fused if fits else shards,
        mesh=mesh,
        in_specs=(
            P(("dp", "seq"), None),
            P(),
            P(None, None, "seq"),
            P(),
            P(),
            P("seq", None),
            P("seq", None),
            P(),
            P("seq", None),
        ),
        out_specs=(P(("dp", "seq"), None), P(("dp", "seq"), None)),
        check_vma=False,
    )
```

```python
import jax
import jax.numpy as jnp
from jax import lax
from jax.experimental import pallas as pl
from jax.experimental.pallas import tpu as pltpu
from jax.sharding import PartitionSpec as P

HEAD_DIM = 128
MESH = pl.DeviceIdType.MESH
MARGIN = 16
EDGE = 8


def beside(z):
    return z + 1 - 2 * lax.rem(z, 2)


def visit(z, k):
    if k == 0:
        return z
    if k == 1:
        return 1 + lax.rem(z, 2)
    if k == 2:
        return lax.rem(2 + 3 * z, 5)
    return 3 * (1 - lax.div(z, 2))


def fused_kernel(
    feat_ref, ngain_ref, cw_ref, bias_ref, again_ref, wq_ref, wkv_ref, scale_ref, wo_ref,
    coarse_ref, attended_ref,
    win, tmp0, tmp1, acc0, acc1, csend, cbuf, wqkv, wout, kvbuf,
    bias8, again8, cw, cwt, scores_ref, prob_ref, cw_sem, act_send, act_recv, wa_send, wa_recv, wb_send, wb_recv, wc_send, wc_recv,
    co_send, co_recv, kv_send, kv_recv,
):
    p = lax.axis_index("dp")
    s = lax.axis_index("seq")
    z, c = lax.div(s, 2), lax.rem(s, 2)
    other = 1 - c
    sibling = (p, 2 * z + other)
    block = feat_ref.shape[0]
    half = block // 2
    heads = scale_ref.shape[0]
    qcols = wq_ref.shape[1]
    taps = cw_ref.shape[0]
    width = cw_ref.shape[1]
    depth = wq_ref.shape[0] // 4
    odepth = wo_ref.shape[0] // 4

    def remote(src, dst, send, recv, device):
        return pltpu.make_async_remote_copy(
            src_ref=src, dst_ref=dst, send_sem=send, recv_sem=recv,
            device_id=device, device_id_type=MESH,
        )

    load = pltpu.make_async_copy(cw_ref, cw, cw_sem)
    load.start()
    barrier = pltpu.get_barrier_semaphore()
    for k in range(1, 8):
        pl.semaphore_signal(
            barrier, inc=1, device_id=(p, lax.rem(s + k, 8)), device_id_type=MESH
        )
    for k in range(1, 4):
        pl.semaphore_signal(
            barrier, inc=1, device_id=(lax.rem(p + k, 4), s), device_id_type=MESH
        )
    wqkv[c, z, :, :qcols] = wq_ref[...]
    wqkv[c, z, :, qcols:] = wkv_ref[...]
    wout[c, z] = wo_ref[...]
    pl.semaphore_wait(barrier, 10)

    started = []

    def qkv_part(cc, zz, pp):
        return wqkv.at[cc, zz, pl.ds(pl.multiple_of(pp * depth, 16), depth), :]

    def out_part(cc, zz, pp):
        return wout.at[cc, zz, pl.ds(pl.multiple_of(pp * odepth, 16), odepth), :]

    parts = (qkv_part, out_part)
    middle = lax.rem(lax.div(z + 1, 2), 2) == 1
    end = (p, 2 * beside(z) + c)
    targets = (2 - lax.div(z, 2), beside(z))

    def relay(ref, send, recv):
        @pl.when(middle)
        def _():
            remote(ref, ref, send, recv, end).start()

    def along_z(n):
        here = parts[n](c, z, p)
        for k, to in enumerate(targets):
            copy = remote(
                here, here, wa_send.at[n, 1 + k], wa_recv.at[n, z], (p, 2 * to + c)
            )
            copy.start()
            started.append(copy)

    def along_dp(n):
        for k in (1, 3, 2):
            zz = visit(z, k)
            here = parts[n](c, zz, p)
            remote(here, here, wa_send.at[n, 0], wa_recv.at[n, zz], sibling).wait_recv()
            if k != 2:
                relay(here, wa_send.at[n, 3 + k // 2], wa_recv.at[n, zz])
            for m in range(1, 4):
                copy = remote(
                    here, here, wb_send.at[n, k, m], wb_recv.at[n, zz, p],
                    (lax.rem(p + m, 4), s),
                )
                copy.start()
                started.append(copy)

    def along_core(n):
        for k in range(1, 4):
            zz = visit(z, k)
            for m in range(1, 4):
                pp = lax.rem(p + m, 4)
                there = parts[n](c, zz, pp)
                remote(
                    there, there, wa_send.at[n, 0], wb_recv.at[n, zz, pp], sibling
                ).wait_recv()
        half_of = (wqkv, wout)[n].at[c]
        copy = remote(half_of, half_of, wc_send.at[n], wc_recv.at[n], sibling)
        copy.start()
        started.append(copy)

    along_z(0)

    x = feat_ref[...].astype(jnp.float32)
    meansq = jnp.mean(x * x, axis=-1, keepdims=True)
    normed = x * lax.rsqrt(meansq + 1e-06) * ngain_ref[...][None, :]
    win[s] = jax.nn.gelu(normed).astype(jnp.bfloat16)
    for k, to in enumerate(targets):
        copy = remote(
            win.at[s], win.at[s], act_send.at[1 + k], act_recv.at[s], (p, 2 * to + c)
        )
        copy.start()
        started.append(copy)
    copy = remote(win.at[s], win.at[s], act_send.at[0], act_recv.at[s], sibling)
    copy.start()
    started.append(copy)

    acc0[...] = jnp.zeros_like(acc0)
    acc1[...] = jnp.zeros_like(acc1)
    tmp0[...] = jnp.zeros_like(tmp0)
    tmp1[...] = jnp.zeros_like(tmp1)

    def convolve_pair(zz):
        rows = win[pl.ds(2 * zz, 2)].reshape(2 * block, win.shape[2])
        for t in range(taps):
            y = jnp.dot(rows, cwt[t], preferred_element_type=jnp.float32)
            tmp0[t, MARGIN : MARGIN + 2 * block, :] = y[:, :128]
            tmp1[t, MARGIN : MARGIN + 2 * block, : width - 128] = y[:, 128:]
        span = 2 * block + 2 * EDGE
        first = MARGIN - EDGE - taps // 2
        at = pl.ds(pl.multiple_of(zz * 2 * block, 8), span)
        for tmp, acc in ((tmp0, acc0), (tmp1, acc1)):
            total = tmp[0, first : first + span, :]
            for t in range(1, taps):
                total = total + tmp[t, first + t : first + t + span, :]
            acc[at, :] += total

    def wait_block(b):
        remote(win.at[b], win.at[b], act_send.at[0], act_recv.at[b], sibling).wait_recv()

    load.wait()
    for t in range(taps):
        cwt[t] = cw[t].T
    bias_row, again_row = bias_ref[...][None, :], again_ref[...][None, :]
    for j in range(8):
        bias8[j] = bias_row[:, j * width : (j + 1) * width]
        again8[j] = again_row[:, j * width : (j + 1) * width]

    def hand_over(k):
        b = 2 * visit(z, k) + c
        return remote(win.at[b], win.at[b], act_send.at[3 + k], act_recv.at[b], sibling)

    def take(k):
        b = 2 * visit(z, k) + c
        wait_block(b)
        if k != 2:
            relay(win.at[b], act_send.at[7 + k // 2], act_recv.at[b])
        hand_over(k).start()

    def step(k):
        if k == 3:
            @pl.when(jnp.logical_not(middle))
            def _():
                wait_block(2 * visit(z, 3) + c)
                hand_over(3).start()

            along_dp(1)
        elif k > 0:
            if k == 2:
                @pl.when(middle)
                def _():
                    take(3)
            take(k)
        wait_block(2 * visit(z, k) + other)
        convolve_pair(visit(z, k))

    def pooled(r, out):
        start = pl.multiple_of(r * block, 8) + EDGE
        bias = bias8[s]
        c0 = jnp.maximum(
            acc0[pl.ds(start, half, stride=2), :], acc0[pl.ds(start + 1, half, stride=2), :]
        )
        c1 = jnp.maximum(
            acc1[pl.ds(start, half, stride=2), :], acc1[pl.ds(start + 1, half, stride=2), :]
        )
        c1 = (c1[:, : width - 128] + bias[:, 128:]).astype(jnp.bfloat16)
        out[:half, :] = (c0 + bias[:, :128]).astype(jnp.bfloat16)
        out[half:, :64] = c1[: half // 2]
        out[half:, 64:] = c1[half // 2 :]

    def send_rows(k, r):
        pooled(r, csend.at[r])
        copy = remote(csend.at[r], cbuf.at[s], co_send.at[k], co_recv.at[s], (p, r))
        copy.start()
        started.append(copy)

    step(0)
    along_dp(0)
    step(1)
    along_z(1)
    step(2)
    upper = lax.div(z, 2)
    send_rows(4, 4 - upper)
    for k in range(1, 4):
        send_rows(k, 4 * upper + lax.rem(s + k, 4))
    pooled(s, cbuf.at[s])
    along_core(0)
    step(3)
    for k in range(5, 8):
        send_rows(k, k + upper * (7 - 2 * k))
    for k in range(1, 8):
        r = lax.rem(s + k, 8)
        remote(csend.at[r], cbuf.at[r], co_send.at[0], co_recv.at[r], sibling).wait_recv()

    squares = jnp.zeros((half, 1), jnp.float32)
    pieces = []
    for j in range(8):
        narrow = jnp.concatenate([cbuf[j, half:, :64], cbuf[j, half:, 64:]], axis=0)
        piece = jnp.concatenate([cbuf[j, :half, :], narrow], axis=1)
        pieces.append(piece)
        piece = piece.astype(jnp.float32)
        squares = squares + jnp.sum(piece * piece, axis=-1, keepdims=True)
    inverse = lax.rsqrt(squares / (8 * width) + 1e-06)

    remote(
        wqkv.at[other], wqkv.at[other], wc_send.at[0], wc_recv.at[0], sibling
    ).wait_recv()
    attn = []
    kv = jnp.zeros((half, wkv_ref.shape[1]), jnp.float32)
    for j in range(8):
        piece = (pieces[j].astype(jnp.float32) * inverse * again8[j]).astype(jnp.bfloat16)
        attn.append(piece)
        kv = kv + jnp.dot(
            piece, wqkv[j % 2, j // 2, :, qcols:], preferred_element_type=jnp.float32
        )
    kvbuf[s] = kv.astype(jnp.bfloat16)
    for k in range(1, 4):
        copy = remote(
            kvbuf.at[s], kvbuf.at[s], kv_send.at[k], kv_recv.at[s], (p, 2 * visit(z, k) + c)
        )
        copy.start()
        started.append(copy)
    copy = remote(kvbuf.at[s], kvbuf.at[s], kv_send.at[0], kv_recv.at[s], sibling)
    copy.start()
    started.append(copy)
    for j in range(8):
        coarse_ref[:, j * width : (j + 1) * width] = pieces[j]
    query = jnp.zeros((half, qcols), jnp.float32)
    for j in range(8):
        query = query + jnp.dot(
            attn[j], wqkv[j % 2, j // 2, :, :qcols], preferred_element_type=jnp.float32
        )
    query = query.astype(jnp.bfloat16)
    stacked = jnp.concatenate(
        [query[:, h * HEAD_DIM : (h + 1) * HEAD_DIM] for h in range(heads)], axis=0
    )
    for k in range(1, 4):
        b = 2 * visit(z, k) + c
        remote(kvbuf.at[b], kvbuf.at[b], kv_send.at[0], kv_recv.at[b], sibling).wait_recv()
        copy = remote(kvbuf.at[b], kvbuf.at[b], kv_send.at[3 + k], kv_recv.at[b], sibling)
        copy.start()
        started.append(copy)
    along_core(1)
    for k in range(4):
        b = 2 * visit(z, k) + other
        remote(kvbuf.at[b], kvbuf.at[b], kv_send.at[0], kv_recv.at[b], sibling).wait_recv()

    keyvals = kvbuf[...].reshape(8 * half, kvbuf.shape[2])
    keys, values = keyvals[:, :HEAD_DIM], keyvals[:, HEAD_DIM:]
    scores_ref[...] = lax.dot_general(
        stacked, keys, (((1,), (1,)), ((), ())), preferred_element_type=jnp.float32
    )
    denoms = []
    for h in range(heads):
        at = slice(h * half, (h + 1) * half)
        scores = scores_ref[at, :] * (scale_ref[h] * HEAD_DIM ** (-0.5))
        expon = jnp.exp(scores - jnp.max(scores, axis=1, keepdims=True))
        denoms.append(jnp.sum(expon, axis=1, keepdims=True))
        prob_ref[at, :] = expon.astype(jnp.bfloat16)
    context = jnp.dot(prob_ref[...], values, preferred_element_type=jnp.float32)
    context = jnp.concatenate(
        [
            (context[h * half : (h + 1) * half] / denoms[h]).astype(jnp.bfloat16)
            for h in [2 * zz + cc for cc in range(2) for zz in range(heads // 2)]
        ],
        axis=1,
    )
    remote(
        wout.at[other], wout.at[other], wc_send.at[1], wc_recv.at[1], sibling
    ).wait_recv()
    attended_ref[...] = jnp.dot(
        context,
        wout[...].reshape(heads * HEAD_DIM, attended_ref.shape[1]),
        preferred_element_type=jnp.float32,
    ).astype(jnp.bfloat16)

    for copy in started:
        copy.wait_send()
    for k in range(1, 4):
        hand_over(k).wait_send()

    @pl.when(middle)
    def _():
        for n in range(2):
            for m in range(3, 5):
                here = parts[n](c, z, p)
                remote(here, here, wa_send.at[n, m], wa_recv.at[n, z], end).wait_send()
        for m in range(7, 9):
            remote(win.at[s], win.at[s], act_send.at[m], act_recv.at[s], end).wait_send()


def fused(
    features, norm_gain, conv_weight, conv_bias, attn_gain,
    query_weight, keyval_weight, head_scale, output_weight,
):
    block, channels = features.shape
    half = block // 2
    taps, _, width = conv_weight.shape
    heads = head_scale.shape[0]
    total = 8 * width
    rows = 8 * block + 2 * EDGE
    qkv_cols = query_weight.shape[1] + keyval_weight.shape[1]
    f32, bf16 = jnp.float32, jnp.bfloat16
    dma = pltpu.SemaphoreType.DMA
    vmem = pl.BlockSpec(memory_space=pltpu.VMEM)
    smem = pl.BlockSpec(memory_space=pltpu.SMEM)
    coarse, attended = pl.pallas_call(
        fused_kernel,
        out_shape=(
            jax.ShapeDtypeStruct((half, total), bf16),
            jax.ShapeDtypeStruct((half, total), bf16),
        ),
        in_specs=[vmem, vmem, pl.BlockSpec(memory_space=pl.ANY)] + [vmem] * 4 + [smem, vmem],
        out_specs=(vmem, vmem),
        scratch_shapes=[
            pltpu.VMEM((8, block, channels), bf16),
            pltpu.VMEM((taps, 2 * block + 2 * MARGIN, 128), f32),
            pltpu.VMEM((taps, 2 * block + 2 * MARGIN, 128), f32),
            pltpu.VMEM((rows, 128), f32),
            pltpu.VMEM((rows, 128), f32),
            pltpu.VMEM((8, half + half // 2, 128), bf16),
            pltpu.VMEM((8, half + half // 2, 128), bf16),
            pltpu.VMEM((2, 4, query_weight.shape[0], qkv_cols), bf16),
            pltpu.VMEM((2, 4) + output_weight.shape, bf16),
            pltpu.VMEM((8, half, keyval_weight.shape[1]), bf16),
            pltpu.VMEM((8, 1, width), f32),
            pltpu.VMEM((8, 1, width), f32),
            pltpu.VMEM((taps, width, channels), bf16),
            pltpu.VMEM((taps, channels, width), bf16),
            pltpu.VMEM((heads * half, 8 * half), f32),
            pltpu.VMEM((heads * half, 8 * half), bf16),
            dma(()),
            dma((9,)), dma((8,)),
            dma((2, 5)), dma((2, 4)),
            dma((2, 4, 4)), dma((2, 4, 4)),
            dma((2,)), dma((2,)),
            dma((8,)), dma((8,)),
            dma((8,)), dma((8,)),
        ],
        compiler_params=pltpu.CompilerParams(
            collective_id=0, has_side_effects=True, vmem_limit_bytes=52 * 1024 * 1024
        ),
    )(
        features,
        norm_gain,
        conv_weight.transpose(0, 2, 1),
        conv_bias,
        attn_gain,
        query_weight,
        keyval_weight,
        head_scale,
        output_weight,
    )
    return coarse, attended


def normalize(values_in, channel_gain):
    meansq = jnp.mean(values_in * values_in, axis=-1, keepdims=True)
    return values_in * lax.rsqrt(meansq + 1e-06) * channel_gain


def convolve(padded, kernel, row_count):
    summed = jnp.zeros((row_count, kernel.shape[2]), jnp.float32)
    for kernel_tap in range(kernel.shape[0]):
        summed = summed + jnp.dot(
            padded[kernel_tap : kernel_tap + row_count],
            kernel[kernel_tap],
            preferred_element_type=jnp.float32,
        )
    return summed


def pool_pairs(levels):
    return jnp.max(levels.reshape(-1, 2, levels.shape[1]), axis=1)


def attend(queries, keyvals, scales):
    row_count = queries.shape[0]
    head_count = scales.shape[0]
    shaped = queries.reshape(row_count, head_count, HEAD_DIM)
    key_block = lax.all_gather(keyvals, "seq", axis=0, tiled=True)
    running_max = jnp.full((head_count, row_count), -1e30, jnp.float32)
    key_part = key_block[:, :HEAD_DIM]
    value_part = key_block[:, HEAD_DIM:]
    scores = (
        jnp.einsum("qhd,kd->hqk", shaped, key_part, preferred_element_type=jnp.float32)
        * scales[:, None, None]
        * HEAD_DIM ** (-0.5)
    )
    newest = jnp.maximum(running_max, jnp.max(scores, axis=2))
    expon = jnp.exp(scores - newest[:, :, None])
    running_sum = jnp.sum(expon, axis=2)
    running_ctx = jnp.einsum(
        "hqk,kd->hqd", expon.astype(jnp.bfloat16), value_part, preferred_element_type=jnp.float32
    )
    context = running_ctx / running_sum[:, :, None]
    return context.transpose(1, 0, 2).reshape(row_count, head_count * HEAD_DIM).astype(jnp.bfloat16)


def shards(
    features,
    norm_gain,
    conv_weight,
    conv_bias,
    attn_gain,
    query_weight,
    keyval_weight,
    head_scale,
    output_weight,
):
    normed = jax.nn.gelu(normalize(features.astype(jnp.float32), norm_gain)).astype(jnp.bfloat16)
    window = lax.all_gather(normed, "seq", axis=0, tiled=True)
    fine_rows = window.shape[0]
    width = conv_weight.shape[0] // 2
    padded = jnp.pad(window, ((width, width), (0, 0)))
    channels = conv_weight.shape[2]
    own_bias = lax.dynamic_slice_in_dim(conv_bias, lax.axis_index("seq") * channels, channels)
    levels = convolve(padded, conv_weight, fine_rows) + own_bias[None, :]
    pooled = pool_pairs(levels).astype(jnp.bfloat16)
    coarse = lax.all_to_all(pooled, "seq", split_axis=0, concat_axis=1, tiled=True)
    attn_in = normalize(coarse.astype(jnp.float32), attn_gain).astype(jnp.bfloat16)
    columns = attn_in
    query_sum = jnp.dot(
        columns,
        lax.all_gather(query_weight, "seq", axis=0, tiled=True),
        preferred_element_type=jnp.float32,
    )
    keyval_sum = jnp.dot(
        columns,
        lax.all_gather(keyval_weight, "seq", axis=0, tiled=True),
        preferred_element_type=jnp.float32,
    )
    queries = query_sum.astype(jnp.bfloat16)
    keyvals = keyval_sum.astype(jnp.bfloat16)
    context = attend(queries, keyvals, head_scale)
    columns = context
    projected = jnp.dot(
        columns,
        lax.all_gather(output_weight, "seq", axis=0, tiled=True),
        preferred_element_type=jnp.float32,
    )
    return (coarse, projected.astype(jnp.bfloat16))


def solution(mesh):
    fits = mesh.shape["dp"] == 4 and mesh.shape["seq"] == 8
    return jax.shard_map(
        fused if fits else shards,
        mesh=mesh,
        in_specs=(
            P(("dp", "seq"), None),
            P(),
            P(None, None, "seq"),
            P(),
            P(),
            P("seq", None),
            P("seq", None),
            P(),
            P("seq", None),
        ),
        out_specs=(P(("dp", "seq"), None), P(("dp", "seq"), None)),
        check_vma=False,
    )
```

```python
import jax
import jax.numpy as jnp
from jax import lax
from jax.experimental import pallas as pl
from jax.experimental.pallas import tpu as pltpu
from jax.sharding import PartitionSpec as P

HEAD_DIM = 128
MESH = pl.DeviceIdType.MESH
MARGIN = 16
EDGE = 8


def nearest(z, k):
    upper = lax.div(z, 2)
    if k == 0:
        return z
    if k == 1:
        return z + 1 - 2 * lax.rem(z, 2)
    return k - upper * (2 * k - 3)


def fused_kernel(
    feat_ref, ngain_ref, cw_ref, bias_ref, again_ref, wq_ref, wkv_ref, scale_ref, wo_ref,
    coarse_ref, attended_ref,
    win, tmp0, tmp1, acc0, acc1, csend, cbuf, wqkv, wout, kvbuf,
    bias8, again8, cw, cwt, scores_ref, prob_ref, cw_sem, act_send, act_recv, wa_send, wa_recv, wb_send, wb_recv, wc_send, wc_recv,
    co_send, co_recv, kv_send, kv_recv,
):
    p = lax.axis_index("dp")
    s = lax.axis_index("seq")
    z, c = lax.div(s, 2), lax.rem(s, 2)
    other = 1 - c
    sibling = (p, 2 * z + other)
    block = feat_ref.shape[0]
    half = block // 2
    heads = scale_ref.shape[0]
    qcols = wq_ref.shape[1]
    taps = cw_ref.shape[0]
    width = cw_ref.shape[1]
    depth = wq_ref.shape[0] // 4
    odepth = wo_ref.shape[0] // 4

    def remote(src, dst, send, recv, device):
        return pltpu.make_async_remote_copy(
            src_ref=src, dst_ref=dst, send_sem=send, recv_sem=recv,
            device_id=device, device_id_type=MESH,
        )

    load = pltpu.make_async_copy(cw_ref, cw, cw_sem)
    load.start()
    barrier = pltpu.get_barrier_semaphore()
    for k in range(1, 8):
        pl.semaphore_signal(
            barrier, inc=1, device_id=(p, lax.rem(s + k, 8)), device_id_type=MESH
        )
    for k in range(1, 4):
        pl.semaphore_signal(
            barrier, inc=1, device_id=(lax.rem(p + k, 4), s), device_id_type=MESH
        )
    wqkv[c, z, :, :qcols] = wq_ref[...]
    wqkv[c, z, :, qcols:] = wkv_ref[...]
    wout[c, z] = wo_ref[...]
    pl.semaphore_wait(barrier, 10)

    started = []

    def qkv_part(cc, zz, pp):
        return wqkv.at[cc, zz, pl.ds(pl.multiple_of(pp * depth, 16), depth), :]

    def out_part(cc, zz, pp):
        return wout.at[cc, zz, pl.ds(pl.multiple_of(pp * odepth, 16), odepth), :]

    parts = (qkv_part, out_part)
    middle = lax.rem(lax.div(z + 1, 2), 2) == 1
    end = (p, 2 * nearest(z, 1) + c)
    relays = []

    def relay(ref, send, recv):
        copy = remote(ref, ref, send, recv, end)
        relays.append(copy)

        @pl.when(middle)
        def _():
            copy.start()

    def along_z(n):
        here = parts[n](c, z, p)
        for k in range(1, 3):
            copy = remote(
                here, here, wa_send.at[n, k], wa_recv.at[n, z], (p, 2 * nearest(z, k) + c)
            )
            copy.start()
            started.append(copy)

    def along_dp(n):
        for k in range(1, 4):
            zz = nearest(z, k)
            here = parts[n](c, zz, p)
            remote(here, here, wa_send.at[n, 0], wa_recv.at[n, zz], sibling).wait_recv()
            if k > 1:
                relay(here, wa_send.at[n, 1 + k], wa_recv.at[n, zz])
            for m in range(1, 4):
                copy = remote(
                    here, here, wb_send.at[n, k, m], wb_recv.at[n, zz, p],
                    (lax.rem(p + m, 4), s),
                )
                copy.start()
                started.append(copy)

    def along_core(n):
        for k in range(1, 4):
            zz = nearest(z, k)
            for m in range(1, 4):
                pp = lax.rem(p + m, 4)
                there = parts[n](c, zz, pp)
                remote(
                    there, there, wa_send.at[n, 0], wb_recv.at[n, zz, pp], sibling
                ).wait_recv()
        half_of = (wqkv, wout)[n].at[c]
        copy = remote(half_of, half_of, wc_send.at[n], wc_recv.at[n], sibling)
        copy.start()
        started.append(copy)

    along_z(0)

    x = feat_ref[...].astype(jnp.float32)
    meansq = jnp.mean(x * x, axis=-1, keepdims=True)
    normed = x * lax.rsqrt(meansq + 1e-06) * ngain_ref[...][None, :]
    win[s] = jax.nn.gelu(normed).astype(jnp.bfloat16)
    copy = remote(win.at[s], win.at[s], act_send.at[0], act_recv.at[s], sibling)
    copy.start()
    started.append(copy)
    for k in range(1, 3):
        copy = remote(
            win.at[s], win.at[s], act_send.at[k], act_recv.at[s], (p, 2 * nearest(z, k) + c)
        )
        copy.start()
        started.append(copy)

    acc0[...] = jnp.zeros_like(acc0)
    acc1[...] = jnp.zeros_like(acc1)
    tmp0[...] = jnp.zeros_like(tmp0)
    tmp1[...] = jnp.zeros_like(tmp1)

    def convolve_pair(zz):
        rows = win[pl.ds(2 * zz, 2)].reshape(2 * block, win.shape[2])
        for t in range(taps):
            y = jnp.dot(rows, cwt[t], preferred_element_type=jnp.float32)
            tmp0[t, MARGIN : MARGIN + 2 * block, :] = y[:, :128]
            tmp1[t, MARGIN : MARGIN + 2 * block, : width - 128] = y[:, 128:]
        span = 2 * block + 2 * EDGE
        first = MARGIN - EDGE - taps // 2
        at = pl.ds(pl.multiple_of(zz * 2 * block, 8), span)
        for tmp, acc in ((tmp0, acc0), (tmp1, acc1)):
            total = tmp[0, first : first + span, :]
            for t in range(1, taps):
                total = total + tmp[t, first + t : first + t + span, :]
            acc[at, :] += total

    def wait_block(b):
        remote(win.at[b], win.at[b], act_send.at[0], act_recv.at[b], sibling).wait_recv()

    load.wait()
    for t in range(taps):
        cwt[t] = cw[t].T
    bias_row, again_row = bias_ref[...][None, :], again_ref[...][None, :]
    for j in range(8):
        bias8[j] = bias_row[:, j * width : (j + 1) * width]
        again8[j] = again_row[:, j * width : (j + 1) * width]

    def step(k):
        zz = nearest(z, k)
        if k > 0:
            b = 2 * zz + c
            wait_block(b)
            copy = remote(
                win.at[b], win.at[b], act_send.at[3 + k], act_recv.at[b], sibling
            )
            if k > 1:
                relay(win.at[b], act_send.at[5 + k], act_recv.at[b])
            copy.start()
            started.append(copy)
        if k == 3:
            along_dp(1)
        wait_block(2 * zz + other)
        convolve_pair(zz)

    def pooled(r, out):
        start = pl.multiple_of(r * block, 8) + EDGE
        bias = bias8[s]
        c0 = jnp.maximum(
            acc0[pl.ds(start, half, stride=2), :], acc0[pl.ds(start + 1, half, stride=2), :]
        )
        c1 = jnp.maximum(
            acc1[pl.ds(start, half, stride=2), :], acc1[pl.ds(start + 1, half, stride=2), :]
        )
        c1 = (c1[:, : width - 128] + bias[:, 128:]).astype(jnp.bfloat16)
        out[:half, :] = (c0 + bias[:, :128]).astype(jnp.bfloat16)
        out[half:, :64] = c1[: half // 2]
        out[half:, 64:] = c1[half // 2 :]

    def send_rows(k, r):
        pooled(r, csend.at[r])
        copy = remote(csend.at[r], cbuf.at[s], co_send.at[k], co_recv.at[s], (p, r))
        copy.start()
        started.append(copy)

    along_dp(0)
    step(0)
    step(1)
    along_z(1)
    step(2)
    upper = lax.div(z, 2)
    send_rows(4, 4 - upper)
    for k in range(1, 4):
        send_rows(k, 4 * upper + lax.rem(s + k, 4))
    pooled(s, cbuf.at[s])
    along_core(0)
    step(3)
    for k in range(5, 8):
        send_rows(k, k + upper * (7 - 2 * k))
    for k in range(1, 8):
        r = lax.rem(s + k, 8)
        remote(csend.at[r], cbuf.at[r], co_send.at[0], co_recv.at[r], sibling).wait_recv()

    squares = jnp.zeros((half, 1), jnp.float32)
    pieces = []
    for j in range(8):
        narrow = jnp.concatenate([cbuf[j, half:, :64], cbuf[j, half:, 64:]], axis=0)
        piece = jnp.concatenate([cbuf[j, :half, :], narrow], axis=1)
        pieces.append(piece)
        piece = piece.astype(jnp.float32)
        squares = squares + jnp.sum(piece * piece, axis=-1, keepdims=True)
    inverse = lax.rsqrt(squares / (8 * width) + 1e-06)

    remote(
        wqkv.at[other], wqkv.at[other], wc_send.at[0], wc_recv.at[0], sibling
    ).wait_recv()
    attn = []
    kv = jnp.zeros((half, wkv_ref.shape[1]), jnp.float32)
    for j in range(8):
        piece = (pieces[j].astype(jnp.float32) * inverse * again8[j]).astype(jnp.bfloat16)
        attn.append(piece)
        kv = kv + jnp.dot(
            piece, wqkv[j % 2, j // 2, :, qcols:], preferred_element_type=jnp.float32
        )
    kvbuf[s] = kv.astype(jnp.bfloat16)
    for k in range(1, 4):
        copy = remote(
            kvbuf.at[s], kvbuf.at[s], kv_send.at[k], kv_recv.at[s], (p, 2 * nearest(z, k) + c)
        )
        copy.start()
        started.append(copy)
    copy = remote(kvbuf.at[s], kvbuf.at[s], kv_send.at[0], kv_recv.at[s], sibling)
    copy.start()
    started.append(copy)
    for j in range(8):
        coarse_ref[:, j * width : (j + 1) * width] = pieces[j]
    query = jnp.zeros((half, qcols), jnp.float32)
    for j in range(8):
        query = query + jnp.dot(
            attn[j], wqkv[j % 2, j // 2, :, :qcols], preferred_element_type=jnp.float32
        )
    query = query.astype(jnp.bfloat16)
    stacked = jnp.concatenate(
        [query[:, h * HEAD_DIM : (h + 1) * HEAD_DIM] for h in range(heads)], axis=0
    )
    for k in range(1, 4):
        b = 2 * nearest(z, k) + c
        remote(kvbuf.at[b], kvbuf.at[b], kv_send.at[0], kv_recv.at[b], sibling).wait_recv()
        copy = remote(kvbuf.at[b], kvbuf.at[b], kv_send.at[3 + k], kv_recv.at[b], sibling)
        copy.start()
        started.append(copy)
    along_core(1)
    for k in range(4):
        b = 2 * nearest(z, k) + other
        remote(kvbuf.at[b], kvbuf.at[b], kv_send.at[0], kv_recv.at[b], sibling).wait_recv()

    keyvals = kvbuf[...].reshape(8 * half, kvbuf.shape[2])
    keys, values = keyvals[:, :HEAD_DIM], keyvals[:, HEAD_DIM:]
    scores_ref[...] = lax.dot_general(
        stacked, keys, (((1,), (1,)), ((), ())), preferred_element_type=jnp.float32
    )
    denoms = []
    for h in range(heads):
        at = slice(h * half, (h + 1) * half)
        scores = scores_ref[at, :] * (scale_ref[h] * HEAD_DIM ** (-0.5))
        expon = jnp.exp(scores - jnp.max(scores, axis=1, keepdims=True))
        denoms.append(jnp.sum(expon, axis=1, keepdims=True))
        prob_ref[at, :] = expon.astype(jnp.bfloat16)
    context = jnp.dot(prob_ref[...], values, preferred_element_type=jnp.float32)
    context = jnp.concatenate(
        [
            (context[h * half : (h + 1) * half] / denoms[h]).astype(jnp.bfloat16)
            for h in [2 * zz + cc for cc in range(2) for zz in range(heads // 2)]
        ],
        axis=1,
    )
    remote(
        wout.at[other], wout.at[other], wc_send.at[1], wc_recv.at[1], sibling
    ).wait_recv()
    attended_ref[...] = jnp.dot(
        context,
        wout[...].reshape(heads * HEAD_DIM, attended_ref.shape[1]),
        preferred_element_type=jnp.float32,
    ).astype(jnp.bfloat16)

    for copy in started:
        copy.wait_send()

    @pl.when(middle)
    def _():
        for copy in relays:
            copy.wait_send()


def fused(
    features, norm_gain, conv_weight, conv_bias, attn_gain,
    query_weight, keyval_weight, head_scale, output_weight,
):
    block, channels = features.shape
    half = block // 2
    taps, _, width = conv_weight.shape
    heads = head_scale.shape[0]
    total = 8 * width
    rows = 8 * block + 2 * EDGE
    qkv_cols = query_weight.shape[1] + keyval_weight.shape[1]
    f32, bf16 = jnp.float32, jnp.bfloat16
    dma = pltpu.SemaphoreType.DMA
    vmem = pl.BlockSpec(memory_space=pltpu.VMEM)
    smem = pl.BlockSpec(memory_space=pltpu.SMEM)
    coarse, attended = pl.pallas_call(
        fused_kernel,
        out_shape=(
            jax.ShapeDtypeStruct((half, total), bf16),
            jax.ShapeDtypeStruct((half, total), bf16),
        ),
        in_specs=[vmem, vmem, pl.BlockSpec(memory_space=pl.ANY)] + [vmem] * 4 + [smem, vmem],
        out_specs=(vmem, vmem),
        scratch_shapes=[
            pltpu.VMEM((8, block, channels), bf16),
            pltpu.VMEM((taps, 2 * block + 2 * MARGIN, 128), f32),
            pltpu.VMEM((taps, 2 * block + 2 * MARGIN, 128), f32),
            pltpu.VMEM((rows, 128), f32),
            pltpu.VMEM((rows, 128), f32),
            pltpu.VMEM((8, half + half // 2, 128), bf16),
            pltpu.VMEM((8, half + half // 2, 128), bf16),
            pltpu.VMEM((2, 4, query_weight.shape[0], qkv_cols), bf16),
            pltpu.VMEM((2, 4) + output_weight.shape, bf16),
            pltpu.VMEM((8, half, keyval_weight.shape[1]), bf16),
            pltpu.VMEM((8, 1, width), f32),
            pltpu.VMEM((8, 1, width), f32),
            pltpu.VMEM((taps, width, channels), bf16),
            pltpu.VMEM((taps, channels, width), bf16),
            pltpu.VMEM((heads * half, 8 * half), f32),
            pltpu.VMEM((heads * half, 8 * half), bf16),
            dma(()),
            dma((9,)), dma((8,)),
            dma((2, 5)), dma((2, 4)),
            dma((2, 4, 4)), dma((2, 4, 4)),
            dma((2,)), dma((2,)),
            dma((8,)), dma((8,)),
            dma((8,)), dma((8,)),
        ],
        compiler_params=pltpu.CompilerParams(
            collective_id=0, has_side_effects=True, vmem_limit_bytes=60 * 1024 * 1024
        ),
    )(
        features,
        norm_gain,
        conv_weight.transpose(0, 2, 1),
        conv_bias,
        attn_gain,
        query_weight,
        keyval_weight,
        head_scale,
        output_weight,
    )
    return coarse, attended


def normalize(values_in, channel_gain):
    meansq = jnp.mean(values_in * values_in, axis=-1, keepdims=True)
    return values_in * lax.rsqrt(meansq + 1e-06) * channel_gain


def convolve(padded, kernel, row_count):
    summed = jnp.zeros((row_count, kernel.shape[2]), jnp.float32)
    for kernel_tap in range(kernel.shape[0]):
        summed = summed + jnp.dot(
            padded[kernel_tap : kernel_tap + row_count],
            kernel[kernel_tap],
            preferred_element_type=jnp.float32,
        )
    return summed


def pool_pairs(levels):
    return jnp.max(levels.reshape(-1, 2, levels.shape[1]), axis=1)


def attend(queries, keyvals, scales):
    row_count = queries.shape[0]
    head_count = scales.shape[0]
    shaped = queries.reshape(row_count, head_count, HEAD_DIM)
    key_block = lax.all_gather(keyvals, "seq", axis=0, tiled=True)
    running_max = jnp.full((head_count, row_count), -1e30, jnp.float32)
    key_part = key_block[:, :HEAD_DIM]
    value_part = key_block[:, HEAD_DIM:]
    scores = (
        jnp.einsum("qhd,kd->hqk", shaped, key_part, preferred_element_type=jnp.float32)
        * scales[:, None, None]
        * HEAD_DIM ** (-0.5)
    )
    newest = jnp.maximum(running_max, jnp.max(scores, axis=2))
    expon = jnp.exp(scores - newest[:, :, None])
    running_sum = jnp.sum(expon, axis=2)
    running_ctx = jnp.einsum(
        "hqk,kd->hqd", expon.astype(jnp.bfloat16), value_part, preferred_element_type=jnp.float32
    )
    context = running_ctx / running_sum[:, :, None]
    return context.transpose(1, 0, 2).reshape(row_count, head_count * HEAD_DIM).astype(jnp.bfloat16)


def shards(
    features,
    norm_gain,
    conv_weight,
    conv_bias,
    attn_gain,
    query_weight,
    keyval_weight,
    head_scale,
    output_weight,
):
    normed = jax.nn.gelu(normalize(features.astype(jnp.float32), norm_gain)).astype(jnp.bfloat16)
    window = lax.all_gather(normed, "seq", axis=0, tiled=True)
    fine_rows = window.shape[0]
    width = conv_weight.shape[0] // 2
    padded = jnp.pad(window, ((width, width), (0, 0)))
    channels = conv_weight.shape[2]
    own_bias = lax.dynamic_slice_in_dim(conv_bias, lax.axis_index("seq") * channels, channels)
    levels = convolve(padded, conv_weight, fine_rows) + own_bias[None, :]
    pooled = pool_pairs(levels).astype(jnp.bfloat16)
    coarse = lax.all_to_all(pooled, "seq", split_axis=0, concat_axis=1, tiled=True)
    attn_in = normalize(coarse.astype(jnp.float32), attn_gain).astype(jnp.bfloat16)
    columns = attn_in
    query_sum = jnp.dot(
        columns,
        lax.all_gather(query_weight, "seq", axis=0, tiled=True),
        preferred_element_type=jnp.float32,
    )
    keyval_sum = jnp.dot(
        columns,
        lax.all_gather(keyval_weight, "seq", axis=0, tiled=True),
        preferred_element_type=jnp.float32,
    )
    queries = query_sum.astype(jnp.bfloat16)
    keyvals = keyval_sum.astype(jnp.bfloat16)
    context = attend(queries, keyvals, head_scale)
    columns = context
    projected = jnp.dot(
        columns,
        lax.all_gather(output_weight, "seq", axis=0, tiled=True),
        preferred_element_type=jnp.float32,
    )
    return (coarse, projected.astype(jnp.bfloat16))


def solution(mesh):
    fits = mesh.shape["dp"] == 4 and mesh.shape["seq"] == 8
    return jax.shard_map(
        fused if fits else shards,
        mesh=mesh,
        in_specs=(
            P(("dp", "seq"), None),
            P(),
            P(None, None, "seq"),
            P(),
            P(),
            P("seq", None),
            P("seq", None),
            P(),
            P("seq", None),
        ),
        out_specs=(P(("dp", "seq"), None), P(("dp", "seq"), None)),
        check_vma=False,
    )
```

```python
import jax
import jax.numpy as jnp
from jax import lax
from jax.experimental import pallas as pl
from jax.experimental.pallas import tpu as pltpu
from jax.sharding import PartitionSpec as P

HEAD_DIM = 128
MESH = pl.DeviceIdType.MESH
MARGIN = 16
EDGE = 8


def nearest(z, k):
    upper = lax.div(z, 2)
    if k == 0:
        return z
    if k == 1:
        return z + 1 - 2 * lax.rem(z, 2)
    return k - upper * (2 * k - 3)


def fused_kernel(
    feat_ref, ngain_ref, cw_ref, bias_ref, again_ref, wq_ref, wkv_ref, scale_ref, wo_ref,
    coarse_ref, attended_ref,
    win, tmp0, tmp1, acc0, acc1, csend, cbuf, wqkv, wout, kvbuf,
    bias8, again8, cw, cwt, scores_ref, prob_ref, cw_sem, act_send, act_recv, wa_send, wa_recv, wb_send, wb_recv, wc_send, wc_recv,
    co_send, co_recv, kv_send, kv_recv,
):
    p = lax.axis_index("dp")
    s = lax.axis_index("seq")
    z, c = lax.div(s, 2), lax.rem(s, 2)
    other = 1 - c
    sibling = (p, 2 * z + other)
    block = feat_ref.shape[0]
    half = block // 2
    heads = scale_ref.shape[0]
    qcols = wq_ref.shape[1]
    taps = cw_ref.shape[0]
    width = cw_ref.shape[1]
    depth = wq_ref.shape[0] // 4
    odepth = wo_ref.shape[0] // 4

    def remote(src, dst, send, recv, device):
        return pltpu.make_async_remote_copy(
            src_ref=src, dst_ref=dst, send_sem=send, recv_sem=recv,
            device_id=device, device_id_type=MESH,
        )

    load = pltpu.make_async_copy(cw_ref, cw, cw_sem)
    load.start()
    barrier = pltpu.get_barrier_semaphore()
    for k in range(1, 8):
        pl.semaphore_signal(
            barrier, inc=1, device_id=(p, lax.rem(s + k, 8)), device_id_type=MESH
        )
    for k in range(1, 4):
        pl.semaphore_signal(
            barrier, inc=1, device_id=(lax.rem(p + k, 4), s), device_id_type=MESH
        )
    wqkv[c, z, :, :qcols] = wq_ref[...]
    wqkv[c, z, :, qcols:] = wkv_ref[...]
    wout[c, z] = wo_ref[...]
    pl.semaphore_wait(barrier, 10)

    started = []

    def qkv_part(cc, zz, pp):
        return wqkv.at[cc, zz, pl.ds(pl.multiple_of(pp * depth, 16), depth), :]

    def out_part(cc, zz, pp):
        return wout.at[cc, zz, pl.ds(pl.multiple_of(pp * odepth, 16), odepth), :]

    parts = (qkv_part, out_part)
    middle = lax.rem(lax.div(z + 1, 2), 2) == 1
    end = (p, 2 * nearest(z, 1) + c)
    relays = []

    def relay(ref, send, recv):
        copy = remote(ref, ref, send, recv, end)
        relays.append(copy)

        @pl.when(middle)
        def _():
            copy.start()

    def along_z(n):
        here = parts[n](c, z, p)
        for k in range(1, 3):
            copy = remote(
                here, here, wa_send.at[n, k], wa_recv.at[n, z], (p, 2 * nearest(z, k) + c)
            )
            copy.start()
            started.append(copy)

    def along_dp(n):
        for k in range(1, 4):
            zz = nearest(z, k)
            here = parts[n](c, zz, p)
            remote(here, here, wa_send.at[n, 0], wa_recv.at[n, zz], sibling).wait_recv()
            if k > 1:
                relay(here, wa_send.at[n, 1 + k], wa_recv.at[n, zz])
            for m in range(1, 4):
                copy = remote(
                    here, here, wb_send.at[n, k, m], wb_recv.at[n, zz, p],
                    (lax.rem(p + m, 4), s),
                )
                copy.start()
                started.append(copy)

    def along_core(n):
        for k in range(1, 4):
            zz = nearest(z, k)
            for m in range(1, 4):
                pp = lax.rem(p + m, 4)
                there = parts[n](c, zz, pp)
                remote(
                    there, there, wa_send.at[n, 0], wb_recv.at[n, zz, pp], sibling
                ).wait_recv()
        half_of = (wqkv, wout)[n].at[c]
        copy = remote(half_of, half_of, wc_send.at[n], wc_recv.at[n], sibling)
        copy.start()
        started.append(copy)

    along_z(0)

    x = feat_ref[...].astype(jnp.float32)
    meansq = jnp.mean(x * x, axis=-1, keepdims=True)
    normed = x * lax.rsqrt(meansq + 1e-06) * ngain_ref[...][None, :]
    win[s] = jax.nn.gelu(normed).astype(jnp.bfloat16)
    copy = remote(win.at[s], win.at[s], act_send.at[0], act_recv.at[s], sibling)
    copy.start()
    started.append(copy)
    for k in range(1, 3):
        copy = remote(
            win.at[s], win.at[s], act_send.at[k], act_recv.at[s], (p, 2 * nearest(z, k) + c)
        )
        copy.start()
        started.append(copy)

    acc0[...] = jnp.zeros_like(acc0)
    acc1[...] = jnp.zeros_like(acc1)
    tmp0[...] = jnp.zeros_like(tmp0)
    tmp1[...] = jnp.zeros_like(tmp1)

    def convolve_pair(zz):
        rows = win[pl.ds(2 * zz, 2)].reshape(2 * block, win.shape[2])
        for t in range(taps):
            y = jnp.dot(rows, cwt[t], preferred_element_type=jnp.float32)
            tmp0[t, MARGIN : MARGIN + 2 * block, :] = y[:, :128]
            tmp1[t, MARGIN : MARGIN + 2 * block, : width - 128] = y[:, 128:]
        span = 2 * block + 2 * EDGE
        first = MARGIN - EDGE - taps // 2
        at = pl.ds(pl.multiple_of(zz * 2 * block, 8), span)
        for tmp, acc in ((tmp0, acc0), (tmp1, acc1)):
            total = tmp[0, first : first + span, :]
            for t in range(1, taps):
                total = total + tmp[t, first + t : first + t + span, :]
            acc[at, :] += total

    def wait_block(b):
        remote(win.at[b], win.at[b], act_send.at[0], act_recv.at[b], sibling).wait_recv()

    load.wait()
    for t in range(taps):
        cwt[t] = cw[t].T
    bias_row, again_row = bias_ref[...][None, :], again_ref[...][None, :]
    for j in range(8):
        bias8[j] = bias_row[:, j * width : (j + 1) * width]
        again8[j] = again_row[:, j * width : (j + 1) * width]

    def step(k):
        zz = nearest(z, k)
        if k > 0:
            b = 2 * zz + c
            wait_block(b)
            copy = remote(
                win.at[b], win.at[b], act_send.at[3 + k], act_recv.at[b], sibling
            )
            if k > 1:
                relay(win.at[b], act_send.at[5 + k], act_recv.at[b])
            copy.start()
            started.append(copy)
        wait_block(2 * zz + other)
        convolve_pair(zz)

    def pooled(r, out):
        start = pl.multiple_of(r * block, 8) + EDGE
        bias = bias8[s]
        c0 = jnp.maximum(
            acc0[pl.ds(start, half, stride=2), :], acc0[pl.ds(start + 1, half, stride=2), :]
        )
        c1 = jnp.maximum(
            acc1[pl.ds(start, half, stride=2), :], acc1[pl.ds(start + 1, half, stride=2), :]
        )
        c1 = (c1[:, : width - 128] + bias[:, 128:]).astype(jnp.bfloat16)
        out[:half, :] = (c0 + bias[:, :128]).astype(jnp.bfloat16)
        out[half:, :64] = c1[: half // 2]
        out[half:, 64:] = c1[half // 2 :]

    def send_rows(k, r):
        pooled(r, csend.at[r])
        copy = remote(csend.at[r], cbuf.at[s], co_send.at[k], co_recv.at[s], (p, r))
        copy.start()
        started.append(copy)

    along_dp(0)
    step(0)
    step(1)
    along_z(1)
    step(2)
    upper = lax.div(z, 2)
    send_rows(4, 4 - upper)
    for k in range(1, 4):
        send_rows(k, 4 * upper + lax.rem(s + k, 4))
    pooled(s, cbuf.at[s])
    along_core(0)
    step(3)
    for k in range(5, 8):
        send_rows(k, k + upper * (7 - 2 * k))
    along_dp(1)
    for k in range(1, 8):
        r = lax.rem(s + k, 8)
        remote(csend.at[r], cbuf.at[r], co_send.at[0], co_recv.at[r], sibling).wait_recv()

    squares = jnp.zeros((half, 1), jnp.float32)
    pieces = []
    for j in range(8):
        narrow = jnp.concatenate([cbuf[j, half:, :64], cbuf[j, half:, 64:]], axis=0)
        piece = jnp.concatenate([cbuf[j, :half, :], narrow], axis=1)
        pieces.append(piece)
        piece = piece.astype(jnp.float32)
        squares = squares + jnp.sum(piece * piece, axis=-1, keepdims=True)
    inverse = lax.rsqrt(squares / (8 * width) + 1e-06)

    remote(
        wqkv.at[other], wqkv.at[other], wc_send.at[0], wc_recv.at[0], sibling
    ).wait_recv()
    attn = []
    kv = jnp.zeros((half, wkv_ref.shape[1]), jnp.float32)
    for j in range(8):
        piece = (pieces[j].astype(jnp.float32) * inverse * again8[j]).astype(jnp.bfloat16)
        attn.append(piece)
        kv = kv + jnp.dot(
            piece, wqkv[j % 2, j // 2, :, qcols:], preferred_element_type=jnp.float32
        )
    kvbuf[s] = kv.astype(jnp.bfloat16)
    for k in range(1, 4):
        copy = remote(
            kvbuf.at[s], kvbuf.at[s], kv_send.at[k], kv_recv.at[s], (p, 2 * nearest(z, k) + c)
        )
        copy.start()
        started.append(copy)
    copy = remote(kvbuf.at[s], kvbuf.at[s], kv_send.at[0], kv_recv.at[s], sibling)
    copy.start()
    started.append(copy)
    for j in range(8):
        coarse_ref[:, j * width : (j + 1) * width] = pieces[j]
    query = jnp.zeros((half, qcols), jnp.float32)
    for j in range(8):
        query = query + jnp.dot(
            attn[j], wqkv[j % 2, j // 2, :, :qcols], preferred_element_type=jnp.float32
        )
    query = query.astype(jnp.bfloat16)
    stacked = jnp.concatenate(
        [query[:, h * HEAD_DIM : (h + 1) * HEAD_DIM] for h in range(heads)], axis=0
    )
    for k in range(1, 4):
        b = 2 * nearest(z, k) + c
        remote(kvbuf.at[b], kvbuf.at[b], kv_send.at[0], kv_recv.at[b], sibling).wait_recv()
        copy = remote(kvbuf.at[b], kvbuf.at[b], kv_send.at[3 + k], kv_recv.at[b], sibling)
        copy.start()
        started.append(copy)
    along_core(1)
    for k in range(4):
        b = 2 * nearest(z, k) + other
        remote(kvbuf.at[b], kvbuf.at[b], kv_send.at[0], kv_recv.at[b], sibling).wait_recv()

    keyvals = kvbuf[...].reshape(8 * half, kvbuf.shape[2])
    keys, values = keyvals[:, :HEAD_DIM], keyvals[:, HEAD_DIM:]
    scores_ref[...] = lax.dot_general(
        stacked, keys, (((1,), (1,)), ((), ())), preferred_element_type=jnp.float32
    )
    denoms = []
    for h in range(heads):
        at = slice(h * half, (h + 1) * half)
        scores = scores_ref[at, :] * (scale_ref[h] * HEAD_DIM ** (-0.5))
        expon = jnp.exp(scores - jnp.max(scores, axis=1, keepdims=True))
        denoms.append(jnp.sum(expon, axis=1, keepdims=True))
        prob_ref[at, :] = expon.astype(jnp.bfloat16)
    context = jnp.dot(prob_ref[...], values, preferred_element_type=jnp.float32)
    context = jnp.concatenate(
        [
            (context[h * half : (h + 1) * half] / denoms[h]).astype(jnp.bfloat16)
            for h in [2 * zz + cc for cc in range(2) for zz in range(heads // 2)]
        ],
        axis=1,
    )
    remote(
        wout.at[other], wout.at[other], wc_send.at[1], wc_recv.at[1], sibling
    ).wait_recv()
    attended_ref[...] = jnp.dot(
        context,
        wout[...].reshape(heads * HEAD_DIM, attended_ref.shape[1]),
        preferred_element_type=jnp.float32,
    ).astype(jnp.bfloat16)

    for copy in started:
        copy.wait_send()

    @pl.when(middle)
    def _():
        for copy in relays:
            copy.wait_send()


def fused(
    features, norm_gain, conv_weight, conv_bias, attn_gain,
    query_weight, keyval_weight, head_scale, output_weight,
):
    block, channels = features.shape
    half = block // 2
    taps, _, width = conv_weight.shape
    heads = head_scale.shape[0]
    total = 8 * width
    rows = 8 * block + 2 * EDGE
    qkv_cols = query_weight.shape[1] + keyval_weight.shape[1]
    f32, bf16 = jnp.float32, jnp.bfloat16
    dma = pltpu.SemaphoreType.DMA
    vmem = pl.BlockSpec(memory_space=pltpu.VMEM)
    smem = pl.BlockSpec(memory_space=pltpu.SMEM)
    coarse, attended = pl.pallas_call(
        fused_kernel,
        out_shape=(
            jax.ShapeDtypeStruct((half, total), bf16),
            jax.ShapeDtypeStruct((half, total), bf16),
        ),
        in_specs=[vmem, vmem, pl.BlockSpec(memory_space=pl.ANY)] + [vmem] * 4 + [smem, vmem],
        out_specs=(vmem, vmem),
        scratch_shapes=[
            pltpu.VMEM((8, block, channels), bf16),
            pltpu.VMEM((taps, 2 * block + 2 * MARGIN, 128), f32),
            pltpu.VMEM((taps, 2 * block + 2 * MARGIN, 128), f32),
            pltpu.VMEM((rows, 128), f32),
            pltpu.VMEM((rows, 128), f32),
            pltpu.VMEM((8, half + half // 2, 128), bf16),
            pltpu.VMEM((8, half + half // 2, 128), bf16),
            pltpu.VMEM((2, 4, query_weight.shape[0], qkv_cols), bf16),
            pltpu.VMEM((2, 4) + output_weight.shape, bf16),
            pltpu.VMEM((8, half, keyval_weight.shape[1]), bf16),
            pltpu.VMEM((8, 1, width), f32),
            pltpu.VMEM((8, 1, width), f32),
            pltpu.VMEM((taps, width, channels), bf16),
            pltpu.VMEM((taps, channels, width), bf16),
            pltpu.VMEM((heads * half, 8 * half), f32),
            pltpu.VMEM((heads * half, 8 * half), bf16),
            dma(()),
            dma((9,)), dma((8,)),
            dma((2, 5)), dma((2, 4)),
            dma((2, 4, 4)), dma((2, 4, 4)),
            dma((2,)), dma((2,)),
            dma((8,)), dma((8,)),
            dma((8,)), dma((8,)),
        ],
        compiler_params=pltpu.CompilerParams(
            collective_id=0, has_side_effects=True, vmem_limit_bytes=60 * 1024 * 1024
        ),
    )(
        features,
        norm_gain,
        conv_weight.transpose(0, 2, 1),
        conv_bias,
        attn_gain,
        query_weight,
        keyval_weight,
        head_scale,
        output_weight,
    )
    return coarse, attended


def normalize(values_in, channel_gain):
    meansq = jnp.mean(values_in * values_in, axis=-1, keepdims=True)
    return values_in * lax.rsqrt(meansq + 1e-06) * channel_gain


def convolve(padded, kernel, row_count):
    summed = jnp.zeros((row_count, kernel.shape[2]), jnp.float32)
    for kernel_tap in range(kernel.shape[0]):
        summed = summed + jnp.dot(
            padded[kernel_tap : kernel_tap + row_count],
            kernel[kernel_tap],
            preferred_element_type=jnp.float32,
        )
    return summed


def pool_pairs(levels):
    return jnp.max(levels.reshape(-1, 2, levels.shape[1]), axis=1)


def attend(queries, keyvals, scales):
    row_count = queries.shape[0]
    head_count = scales.shape[0]
    shaped = queries.reshape(row_count, head_count, HEAD_DIM)
    key_block = lax.all_gather(keyvals, "seq", axis=0, tiled=True)
    running_max = jnp.full((head_count, row_count), -1e30, jnp.float32)
    key_part = key_block[:, :HEAD_DIM]
    value_part = key_block[:, HEAD_DIM:]
    scores = (
        jnp.einsum("qhd,kd->hqk", shaped, key_part, preferred_element_type=jnp.float32)
        * scales[:, None, None]
        * HEAD_DIM ** (-0.5)
    )
    newest = jnp.maximum(running_max, jnp.max(scores, axis=2))
    expon = jnp.exp(scores - newest[:, :, None])
    running_sum = jnp.sum(expon, axis=2)
    running_ctx = jnp.einsum(
        "hqk,kd->hqd", expon.astype(jnp.bfloat16), value_part, preferred_element_type=jnp.float32
    )
    context = running_ctx / running_sum[:, :, None]
    return context.transpose(1, 0, 2).reshape(row_count, head_count * HEAD_DIM).astype(jnp.bfloat16)


def shards(
    features,
    norm_gain,
    conv_weight,
    conv_bias,
    attn_gain,
    query_weight,
    keyval_weight,
    head_scale,
    output_weight,
):
    normed = jax.nn.gelu(normalize(features.astype(jnp.float32), norm_gain)).astype(jnp.bfloat16)
    window = lax.all_gather(normed, "seq", axis=0, tiled=True)
    fine_rows = window.shape[0]
    width = conv_weight.shape[0] // 2
    padded = jnp.pad(window, ((width, width), (0, 0)))
    channels = conv_weight.shape[2]
    own_bias = lax.dynamic_slice_in_dim(conv_bias, lax.axis_index("seq") * channels, channels)
    levels = convolve(padded, conv_weight, fine_rows) + own_bias[None, :]
    pooled = pool_pairs(levels).astype(jnp.bfloat16)
    coarse = lax.all_to_all(pooled, "seq", split_axis=0, concat_axis=1, tiled=True)
    attn_in = normalize(coarse.astype(jnp.float32), attn_gain).astype(jnp.bfloat16)
    columns = attn_in
    query_sum = jnp.dot(
        columns,
        lax.all_gather(query_weight, "seq", axis=0, tiled=True),
        preferred_element_type=jnp.float32,
    )
    keyval_sum = jnp.dot(
        columns,
        lax.all_gather(keyval_weight, "seq", axis=0, tiled=True),
        preferred_element_type=jnp.float32,
    )
    queries = query_sum.astype(jnp.bfloat16)
    keyvals = keyval_sum.astype(jnp.bfloat16)
    context = attend(queries, keyvals, head_scale)
    columns = context
    projected = jnp.dot(
        columns,
        lax.all_gather(output_weight, "seq", axis=0, tiled=True),
        preferred_element_type=jnp.float32,
    )
    return (coarse, projected.astype(jnp.bfloat16))


def solution(mesh):
    fits = mesh.shape["dp"] == 4 and mesh.shape["seq"] == 8
    return jax.shard_map(
        fused if fits else shards,
        mesh=mesh,
        in_specs=(
            P(("dp", "seq"), None),
            P(),
            P(None, None, "seq"),
            P(),
            P(),
            P("seq", None),
            P("seq", None),
            P(),
            P("seq", None),
        ),
        out_specs=(P(("dp", "seq"), None), P(("dp", "seq"), None)),
        check_vma=False,
    )
```
